256 devices in a mesh: dp: 8 (over y, core), expert: 32 (over x, z).
Axes of the slice: x: 4, y: 4, z: 8, core: 2. Of those that a mesh axis runs over, the one named last changes fastest.
Arguments:
- inputs: bfloat16 [512, 2304], P('dp'), may hold values from -90 to 90
- tail_inputs: bfloat16 [256, 2304], P('dp'), may hold values from -90 to 90
- states: bfloat16 [512, 32, 128, 128], P('dp', 'expert'), may hold values from -18 to 18
- tail_ids: int32 [256], replicated, may hold values from 0 to 511, as said below
- routes: int32 [512, 8], replicated, may hold values from 0 to 127, all different within a row; in each aligned block of 64 rows (0 to 63, 64 to 127, ...) at most 8 rows name the same one
- tail_routes: int32 [256, 8], replicated, may hold values from 0 to 127, all different within a row; in each aligned block of 32 rows (0 to 31, 32 to 63, ...) at most 4 rows name the same one
- attention_gain: float32 [2304], replicated, may hold values from 0.1 to 1.9
- query_weight: bfloat16 [2304, 4096], P(None, 'expert'), may hold values from -0.125 to 0.125
- key_weight: bfloat16 [2304, 4096], P(None, 'expert'), may hold values from -0.125 to 0.125
- value_weight: bfloat16 [2304, 4096], P(None, 'expert'), may hold values from -0.125 to 0.125
- decay_down: bfloat16 [2304, 128], replicated, may hold values from -0.125 to 0.125
- decay_up: bfloat16 [128, 4096], P(None, 'expert'), may hold values from -0.5 to 0.5
- decay_bias: float32 [4096], P('expert'), may hold values from -4 to 4
- decay_log: float32 [32], P('expert'), may hold values from -3 to 0.5
- beta_weight: bfloat16 [2304, 32], P(None, 'expert'), may hold values from -0.125 to 0.125
- output_gain: float32 [128], replicated, may hold values from 0.1 to 1.9
- head_out: bfloat16 [4096, 2304], P('expert'), may hold values from -0.09375 to 0.09375
- expert_gain: float32 [2304], replicated, may hold values from 0.1 to 1.9
- router_weight: bfloat16 [2304, 128], replicated, may hold values from -0.125 to 0.125
- gate_weight: bfloat16 [128, 2304, 1024], P('expert', None, 'dp'), may hold values from -0.125 to 0.125
- up_weight: bfloat16 [128, 2304, 1024], P('expert', None, 'dp'), may hold values from -0.125 to 0.125
- down_weight: bfloat16 [128, 1024, 2304], P('expert', 'dp'), may hold values from -0.1875 to 0.1875
Outputs:
- first_out: bfloat16 [512, 2304], P(('dp', 'expert'))
- tail_out: bfloat16 [256, 2304], P(('dp', 'expert'))
The draws below stay inside these ranges and needn't reach their ends.
Inputs may be any that keep to these rules, and one draw needn't show every extreme that they name: `tail_ids`: distinct row ids. Position p belongs to destination group p // 32; a destination's 32 positions form 4 aligned runs of 8, each run from one source group (id // 64), the four sources distinct, so at most 8 tail rows go from one group to another and that count is reached. `routes`: in each aligned block of 64 rows (one group's rows) no expert is named by more than 8 rows, and that count is reached. `tail_routes`: in each aligned block of 32 rows no expert is named by more than 4 rows, and that count is reached.
All inputs are finite; a program needn't handle non-finite values.
Results may differ from the reference program's by a relative error of at most 0.015.
Values may be sent and summed in bfloat16 or wider, within the bound.
A program may use at most 128 MiB of HBM per device.

```python
import math
import jax
import jax.numpy as jnp
import numpy as np
from jax import lax

D = 2304
HDIM = 128
MOE_FF = 1024
TOPK = 8
R_DEV = 64
HEADS = 32
EXPERTS = 128
TAIL_DEV = 32
ROWS = 512
TAIL = 256
CAPT = 8
CAPE = 8
CAPE2 = 4
N_DP = 8


def scaled_rows(key, base, row_lo, row_hi, col_lo, col_hi):
    row_key, col_key = jax.random.split(key)
    row_scale = jnp.exp(jax.random.uniform(row_key, base.shape[:-1] + (1,), minval=math.log(row_lo), maxval=math.log(row_hi)))
    col_scale = jnp.exp(jax.random.uniform(col_key, (base.shape[-1],), minval=math.log(col_lo), maxval=math.log(col_hi)))
    return base * row_scale * col_scale


def draw_inputs(key, part):
    key = jax.random.fold_in(key, 3)
    base_key, scale_key = jax.random.split(key)
    base = jnp.clip(jax.random.normal(base_key, (ROWS, D)), -6.0, 6.0)
    return scaled_rows(scale_key, base, 0.5, 5.0, 0.3, 3.0).astype(jnp.bfloat16)


def draw_tail_inputs(key, part):
    key = jax.random.fold_in(key, 5)
    base_key, scale_key = jax.random.split(key)
    base = jnp.clip(jax.random.normal(base_key, (TAIL, D)), -6.0, 6.0)
    return scaled_rows(scale_key, base, 0.5, 5.0, 0.3, 3.0).astype(jnp.bfloat16)


def draw_states(key, part):
    key = jax.random.fold_in(key, 7)
    base_key, scale_key = jax.random.split(key)
    base = 0.5 * jnp.clip(jax.random.normal(base_key, (ROWS, HEADS, HDIM, HDIM)), -6.0, 6.0)
    return scaled_rows(scale_key, base, 0.3, 3.0, 0.5, 2.0).astype(jnp.bfloat16)


def draw_tail_ids(key, part):
    key = jax.random.fold_in(key, 11)
    order_key, rows_key = jax.random.split(key)
    order = jax.random.permutation(order_key, N_DP)
    destinations = jnp.arange(N_DP, dtype=jnp.int32)[:, None]
    run_number = jnp.arange(4, dtype=jnp.int32)[None, :]
    others = N_DP - 2
    other_slot = (destinations + run_number - 2) % others
    source_place = jnp.where(run_number < 2, run_number, 2 + other_slot)
    sources = order[source_place].reshape(-1)
    pair_count = sources.shape[0]
    same_source = sources[:, None] == sources[None, :]
    earlier = jnp.arange(pair_count)[None, :] < jnp.arange(pair_count)[:, None]
    ranked = jnp.sum((same_source & earlier).astype(jnp.int32), axis=1)
    row_orders = jax.vmap(lambda row_key: jax.random.permutation(row_key, R_DEV))(jax.random.split(rows_key, N_DP))
    within = jnp.arange(CAPT, dtype=jnp.int32)
    local_rows = row_orders[sources[:, None], ranked[:, None] * CAPT + within[None, :]]
    global_rows = sources[:, None] * R_DEV + local_rows
    return global_rows.reshape(TAIL).astype(jnp.int32)


def levels(stream_key, dims, shards, low, largest):
    def one(dim, parts):
        steps = jax.random.uniform(jax.random.fold_in(jax.random.fold_in(stream_key, 6), dim), (parts,), jnp.float32, low / len(shards), largest / len(shards))
        return jnp.repeat(jnp.exp(steps), dims[dim] // parts).reshape((-1,) + (1,) * (len(dims) - dim - 1))

    level = one(*shards[0])
    for cut in shards[1:]:
        level = level * one(*cut)
    return level


def routed_block(own_key, own, number, rows, number_of, top, most, skew):
    order = jax.random.permutation(own_key, number_of)
    heavy_load, ordinary = portions_of(number_of, rows * top, most, skew, True), portions_of(number_of, rows * top, most, skew, False)
    places = jnp.arange(number_of)

    def named(lengths, rotation):
        used = int((lengths > 0).sum())
        fixed = max(1, used // 4)
        moved = fixed + (places - fixed + rotation * (used - fixed)) % max(1, number_of - fixed)
        return jnp.zeros((number_of,), jnp.int32).at[order[jnp.where(places < fixed, places, moved)]].set(jnp.asarray(lengths, jnp.int32))

    lengths = jnp.where(number % 4 == 0, named(heavy_load, number // 4), named(ordinary, number - number // 4 - 1))
    mixed = jax.random.permutation(jax.random.fold_in(own, 3), number_of)
    donor, receiver = mixed[0:number_of // 2 * 2:2], mixed[1:number_of // 2 * 2:2]
    margin = jnp.minimum(lengths[donor] - 1, most - lengths[receiver]) // 2
    margin = jnp.where((donor == order[0]) | (receiver == order[0]) | (lengths[receiver] == 0), 0, jnp.maximum(margin, 0))
    moved = jax.random.randint(jax.random.fold_in(own, 4), (number_of // 2,), 0, 1 << 20) % (margin + 1)
    lengths = lengths.at[donor].add(-moved).at[receiver].add(moved)
    members = jnp.searchsorted(jnp.cumsum(lengths), jnp.arange(rows * top), side="right").astype(jnp.int32)
    table = members.reshape(top, rows).T
    table = table[jax.random.permutation(jax.random.fold_in(own, 1), rows)]
    rotation = jax.random.randint(jax.random.fold_in(own, 2), (rows, 1), 0, top)
    return jnp.take_along_axis(table, (jnp.arange(top)[None, :] + rotation) % top, axis=1)


def portions_of(number_of, total, most, slope, full):
    weights = [(1 << 20) // math.isqrt(standing ** slope) + 1 for standing in range(1, number_of + 1)]
    largest = most if full else min(most, max(-(-total // number_of), total * weights[0] // sum(weights)))
    least = 1 if total - largest >= number_of - 1 else 0
    given, rest = [largest] + [least] * (number_of - 1), total - largest - least * (number_of - 1)
    while rest > 0:
        free = [i for i in range(1, number_of) if given[i] < largest] or [i for i in range(1, number_of) if given[i] < most]
        pool, left = sum([weights[i] for i in free]), rest
        for i in free:
            extra = min(most - given[i], max(1, left * weights[i] // pool), rest)
            given[i] = given[i] + extra
            rest = rest - extra
    return np.array(given)


def noise(rng, extent, spread, bound, pieces=(), kind=jnp.bfloat16):
    values = jax.random.normal(rng, extent, jnp.float32) * spread
    if len(pieces) > 0:
        values = levels(rng, extent, pieces, -0.22, 0.18) * values
    return jnp.clip(values, min=-bound, max=bound).astype(kind)


def setup_inputs(seed: int = 0) -> dict:
    key_list = jax.random.split(jax.random.key(seed), 23)
    inputs = draw_inputs(jax.random.fold_in(key_list[22], 71), 0)
    tail_inputs = draw_tail_inputs(jax.random.fold_in(key_list[22], 71), 0)
    states = draw_states(jax.random.fold_in(key_list[22], 71), 0)
    tail_ids = draw_tail_ids(jax.random.fold_in(key_list[22], 71), 0)
    routes_keys = jax.random.split(jax.random.fold_in(key_list[4], 1), ROWS // R_DEV)
    routes_turns = jax.random.permutation(jax.random.fold_in(key_list[4], 3), ROWS // R_DEV)
    routes = jax.vmap(lambda own, number: routed_block(jax.random.fold_in(key_list[4], 2), own, number, R_DEV, EXPERTS, TOPK, CAPE, 2))(routes_keys, routes_turns).reshape((ROWS, TOPK))
    tail_routes_keys = jax.random.split(jax.random.fold_in(key_list[5], 1), TAIL // TAIL_DEV)
    tail_routes_turns = jax.random.permutation(jax.random.fold_in(key_list[5], 3), TAIL // TAIL_DEV)
    tail_routes = jax.vmap(lambda own, number: routed_block(jax.random.fold_in(key_list[5], 2), own, number, TAIL_DEV, EXPERTS, TOPK, CAPE2, 2))(tail_routes_keys, tail_routes_turns).reshape((TAIL, TOPK))
    attention_gain = jnp.clip(1.0 + 0.18 * jax.random.normal(key_list[6], (D,), jnp.float32), 0.1, 1.9)
    query_weight = noise(key_list[7], (D, HEADS * HDIM), D ** -0.5, 0.125, ((1, 32),))
    key_weight = noise(key_list[8], (D, HEADS * HDIM), D ** -0.5, 0.125, ((1, 32),))
    value_weight = noise(key_list[9], (D, HEADS * HDIM), D ** -0.5, 0.125, ((1, 32),))
    decay_down = noise(key_list[10], (D, HDIM), D ** -0.5, 0.125)
    decay_up = noise(key_list[11], (HDIM, HEADS * HDIM), HDIM ** -0.5, 0.5, ((1, 32),))
    decay_bias = noise(key_list[12], (HEADS * HDIM,), 1.0, 4.0, ((0, 32),), jnp.float32)
    decay_log = jnp.clip(-3.0 + 3.5 * jax.random.uniform(key_list[13], (HEADS,), jnp.float32) ** levels(key_list[13], (HEADS,), ((0, 32),), -0.2, 0.2), -3.0, 0.5)
    beta_weight = noise(key_list[14], (D, HEADS), D ** -0.5, 0.125, ((1, 32),))
    output_gain = jnp.clip(1.0 + 0.18 * jax.random.normal(key_list[15], (HDIM,), jnp.float32), 0.1, 1.9)
    head_out = noise(key_list[16], (HEADS * HDIM, D), (HEADS * HDIM) ** -0.5, 0.09375, ((0, 32),))
    expert_gain = jnp.clip(1.0 + 0.18 * jax.random.normal(key_list[17], (D,), jnp.float32), 0.1, 1.9)
    router_weight = noise(key_list[18], (D, EXPERTS), D ** -0.5, 0.125)
    gate_weight = noise(key_list[19], (EXPERTS, D, MOE_FF), D ** -0.5, 0.125, ((0, 32), (2, 8)))
    up_weight = noise(key_list[20], (EXPERTS, D, MOE_FF), D ** -0.5, 0.125, ((0, 32), (2, 8)))
    down_weight = noise(key_list[21], (EXPERTS, MOE_FF, D), MOE_FF ** -0.5, 0.1875, ((0, 32), (1, 8)))
    return dict(inputs=inputs, tail_inputs=tail_inputs, states=states, tail_ids=tail_ids, routes=routes, tail_routes=tail_routes, attention_gain=attention_gain, query_weight=query_weight, key_weight=key_weight, value_weight=value_weight, decay_down=decay_down, decay_up=decay_up, decay_bias=decay_bias, decay_log=decay_log, beta_weight=beta_weight, output_gain=output_gain, head_out=head_out, expert_gain=expert_gain, router_weight=router_weight, gate_weight=gate_weight, up_weight=up_weight, down_weight=down_weight)


epsilon = 1e-06
route_scale = 2.446
exact_mode = lax.Precision.HIGHEST

def rms_rows(source, gain):
    wide = source.astype(jnp.float32)
    factor = lax.rsqrt(lax.optimization_barrier(jnp.mean(wide * wide, axis=-1, keepdims=True)) + epsilon)
    return (wide * factor * gain.astype(jnp.float32)).astype(jnp.bfloat16)

def unit_rows(source):
    return source * lax.rsqrt(lax.optimization_barrier(jnp.sum(source * source, axis=-1, keepdims=True)) + epsilon)

def delta_step(normed, state_rows, layer):
    attention_gain, query_weight, key_weight, value_weight, decay_down, decay_up, decay_bias, decay_log, beta_weight, output_gain, head_out = layer
    row_count = normed.shape[0]
    head_count = state_rows.shape[1]
    head_width = state_rows.shape[2]

    def project(weight):
        produced = jnp.dot(normed, weight, preferred_element_type=jnp.float32)
        return jax.nn.silu(produced).reshape(row_count, head_count, head_width)
    query_rows = unit_rows(project(query_weight))
    key_rows = unit_rows(project(key_weight))
    value_rows = project(value_weight)
    lowrank = jnp.dot(normed, decay_down, preferred_element_type=jnp.float32).astype(jnp.bfloat16)
    gate_input = jnp.dot(lowrank, decay_up, preferred_element_type=jnp.float32) + decay_bias
    decay_rate = jnp.exp(decay_log)[None, :, None] * jax.nn.softplus(gate_input.reshape(row_count, head_count, head_width))
    decay_rows = jnp.exp(-decay_rate)
    beta_rows = jax.nn.sigmoid(jnp.dot(normed, beta_weight, preferred_element_type=jnp.float32))
    kept_state = decay_rows[..., None] * state_rows.astype(jnp.float32)
    recalled = jnp.einsum('rhkv,rhk->rhv', kept_state, key_rows, precision=exact_mode)
    update = (beta_rows[..., None] * key_rows)[..., None] * (value_rows - recalled)[..., None, :]
    fresh_state = kept_state + update
    readout = jnp.einsum('rhkv,rhk->rhv', fresh_state, query_rows, precision=exact_mode) * head_width ** (-0.5)
    normed_out = readout * lax.rsqrt(lax.optimization_barrier(jnp.mean(readout * readout, axis=-1, keepdims=True)) + epsilon)
    normed_out = normed_out * output_gain.astype(jnp.float32)
    return (normed_out.astype(jnp.bfloat16).reshape(row_count, head_count * head_width), fresh_state)

def attention_layer(tokens, state_rows, layer):
    normed = rms_rows(tokens, layer[0])
    block_count = tokens.shape[0] // 16

    def one_block(paired):
        normed_block, state_block = paired
        head_rows, fresh_state = delta_step(normed_block, state_block, layer)
        produced = jnp.dot(head_rows, layer[10], preferred_element_type=jnp.float32)
        return (produced, fresh_state.astype(jnp.bfloat16))
    produced, fresh = lax.map(one_block, (normed.reshape(block_count, 16, tokens.shape[1]), state_rows.reshape((block_count, 16) + state_rows.shape[1:])))
    hidden = (tokens.astype(jnp.float32) + produced.reshape(tokens.shape)).astype(jnp.bfloat16)
    return (hidden, fresh.reshape(state_rows.shape))

def expert_layer(hidden, route_table, experts, capacity):
    expert_gain, router_weight, gate_weight, up_weight, down_weight = experts
    normed = rms_rows(hidden, expert_gain)
    logits = jnp.dot(normed, router_weight, preferred_element_type=jnp.float32)
    scores = jax.nn.sigmoid(logits)
    chosen = jnp.take_along_axis(scores, route_table, axis=1)
    shares = route_scale * chosen / lax.optimization_barrier(jnp.sum(chosen, axis=1, keepdims=True))
    limit = capacity * N_DP

    def one_expert(summed, expert_id):
        named_rows = route_table == expert_id
        weight_rows = lax.optimization_barrier(jnp.sum(jnp.where(named_rows, shares, 0.0), axis=1))
        present = jnp.any(named_rows, axis=1)
        found = jnp.nonzero(present, size=limit, fill_value=0)[0]
        usable = jnp.arange(limit) < jnp.sum(present.astype(jnp.int32))
        picked = normed[found]
        gate_rows = jnp.dot(picked, gate_weight[expert_id], preferred_element_type=jnp.float32)
        up_rows = jnp.dot(picked, up_weight[expert_id], preferred_element_type=jnp.float32)
        active = (jax.nn.silu(gate_rows) * up_rows).astype(jnp.bfloat16)
        produced = jnp.dot(active, down_weight[expert_id], preferred_element_type=jnp.float32)
        factor = jnp.where(usable, weight_rows[found], 0.0)
        return (summed.at[found].add(factor[:, None] * produced), None)
    summed, unused = lax.scan(one_expert, jnp.zeros(hidden.shape, jnp.float32), jnp.arange(router_weight.shape[1], dtype=jnp.int32))
    return (hidden.astype(jnp.float32) + summed).astype(jnp.bfloat16)

def reference(inputs, tail_inputs, states, tail_ids, routes, tail_routes, attention_gain, query_weight, key_weight, value_weight, decay_down, decay_up, decay_bias, decay_log, beta_weight, output_gain, head_out, expert_gain, router_weight, gate_weight, up_weight, down_weight):
    layer = (attention_gain, query_weight, key_weight, value_weight, decay_down, decay_up, decay_bias, decay_log, beta_weight, output_gain, head_out)
    experts = (expert_gain, router_weight, gate_weight, up_weight, down_weight)
    first_hidden, stored = attention_layer(inputs, states, layer)
    first_out = expert_layer(first_hidden, routes, experts, CAPE)
    tail_state = jnp.take(stored, tail_ids, axis=0)
    tail_hidden, unused = attention_layer(tail_inputs, tail_state, layer)
    tail_out = expert_layer(tail_hidden, tail_routes, experts, CAPE2)
    return (first_out, tail_out)
```

```python
import functools

import jax
import jax.numpy as jnp
from jax import lax
from jax.experimental import pallas as pl
from jax.experimental.pallas import tpu as pltpu
from jax.sharding import PartitionSpec as P

F32 = jnp.float32
BF16 = jnp.bfloat16
EPS = 1e-06
ROUTE_SCALE = 2.446
MESH = pl.DeviceIdType.MESH
VMEM_LIMIT = 48 * 1024 * 1024
D = 2304
H = 128
NCT = D // 128
R1 = 64
R2 = 32
RT = R1 + R2
SLOTS = 48
NE = 32
ND = 8
NOWN = 27


def iota(shape, dim):
    return lax.broadcasted_iota(jnp.int32, shape, dim)


def dot(a, b, contract=((1,), (0,)), precision=None):
    return lax.dot_general(
        a, b, (contract, ((), ())), precision=precision, preferred_element_type=F32
    )


def rms(wide, gain):
    factor = lax.rsqrt(jnp.mean(wide * wide, axis=-1, keepdims=True) + EPS)
    return wide * factor * gain


def rcopy(src, dst, send, recv, axis, index):
    return pltpu.make_async_remote_copy(
        src_ref=src,
        dst_ref=dst,
        send_sem=send,
        recv_sem=recv,
        device_id={axis: index},
        device_id_type=MESH,
    )


def greet(axes):
    barrier = pltpu.get_barrier_semaphore()
    total = 0
    for axis, size in axes:
        me = lax.axis_index(axis)

        def tell(k, carry):
            pl.semaphore_signal(
                barrier,
                inc=1,
                device_id={axis: lax.rem(me + k, size)},
                device_id_type=MESH,
            )
            return carry

        lax.fori_loop(1, size, tell, 0)
        total += size - 1
    pl.semaphore_wait(barrier, total)


def project_kernel(
    x1, x2, gain, wq, wk, wv, wdd, wdu, bias, dlog, wb, p1, p2, normed
):
    normed[0:R1, :] = rms(x1[...].astype(F32), gain[...]).astype(BF16)
    normed[R1:RT, :] = rms(x2[...].astype(F32), gain[...]).astype(BF16)
    n = normed[...]

    def project(w):
        produced = dot(n, w[...])
        return produced * jax.nn.sigmoid(produced)

    def unit(v):
        return v * lax.rsqrt(jnp.sum(v * v, axis=-1, keepdims=True) + EPS)

    q = unit(project(wq))
    k = unit(project(wk))
    v = project(wv)
    low = dot(n, wdd[...]).astype(BF16)
    gate = dot(low, wdu[...]) + bias[...]
    soft = jnp.maximum(gate, 0.0) + jnp.log(1.0 + jnp.exp(-jnp.abs(gate)))
    strength = jnp.exp(jnp.full((RT, H), dlog[0], F32))
    decay = jnp.exp(-(strength * soft))
    beta = jax.nn.sigmoid(
        jnp.sum(n.astype(F32) * wb[...].astype(F32), axis=-1, keepdims=True)
    )
    dk = decay * k
    dq = decay * q
    s = jnp.broadcast_to(beta * jnp.sum(k * q, axis=-1, keepdims=True), (RT, H))
    dk_hi = dk.astype(BF16).astype(F32)
    dq_hi = dq.astype(BF16).astype(F32)
    parts = (dk_hi, dk - dk_hi, dq_hi, dq - dq_hi, v, s, decay, beta * k)
    for c, part in enumerate(parts):
        p1[:, c * H : (c + 1) * H] = part[0:R1, :]
    for c, part in enumerate((dk, dq, v, s)):
        p2[:, c * H : (c + 1) * H] = part[R1:RT, :].astype(BF16)


def share_kernel(p2, out, send, recv, local):
    me = lax.axis_index("dp")
    greet((("dp", ND),))
    own = pltpu.make_async_copy(p2, out.at[me], local)
    own.start()

    def start(k, carry):
        peer = lax.rem(me + k, ND)
        rcopy(p2, out.at[me], send.at[peer], recv.at[me], "dp", peer).start()
        return carry

    def finish(k, carry):
        peer = lax.rem(me + k, ND)
        copy = rcopy(p2, out.at[peer], send.at[peer], recv.at[peer], "dp", peer)
        copy.wait_send()
        copy.wait_recv()
        return carry

    lax.fori_loop(1, ND, start, 0)
    lax.fori_loop(1, ND, finish, 0)
    own.wait()


def attend_kernel(p1, p2, st, ids, og, h1, h2, named, tp, h1s, h2s, ro1, ro2):
    i = pl.program_id(0)

    @pl.when(i == 0)
    def _():
        base = lax.axis_index("dp") * R1
        named[...] = (ids[...] == base + iota((R1, 256), 0)).astype(F32)
        tp[...] = dot(named[...].astype(BF16), p2[...])

    m = iota((16, H), 0)
    t2 = tp[pl.ds(pl.multiple_of(i * 8, 8), 8), :]
    dcol = jnp.transpose(p1[:, 6 * H : 7 * H])
    bcol = jnp.transpose(p1[:, 7 * H : 8 * H])
    for j in range(8):

        def row(c):
            return p1[j : j + 1, c * H : (c + 1) * H]

        def row2(c):
            return t2[j : j + 1, c * H : (c + 1) * H]

        state = st[j]
        a = jnp.where(m == 0, row(0), jnp.where(m == 1, row(1), jnp.where(m == 2, row(2), row(3))))
        got = dot(a.astype(BF16), state)
        u = row(4) - (got[0:1] + got[1:2])
        ro1[j : j + 1, :] = got[2:3] + got[3:4] + row(5) * u
        fresh = state.astype(F32) * dcol[:, j : j + 1] + bcol[:, j : j + 1] * u
        a2 = jnp.where(m == 0, row2(0), row2(1))
        got2 = dot(a2.astype(BF16), fresh.astype(BF16))
        u2 = row2(2) - got2[0:1]
        ro2[j : j + 1, :] = got2[1:2] + row2(3) * u2
    rows = pl.ds(pl.multiple_of(i * 8, 8), 8)
    h1s[rows, :] = rms(ro1[...] * H**-0.5, og[...])
    h2s[rows, :] = rms(ro2[...] * H**-0.5, og[...])

    @pl.when(i == pl.num_programs(0) - 1)
    def _():
        h1[...] = h1s[...].astype(BF16)
        h2[...] = dot(
            named[...].astype(BF16), h2s[...].astype(BF16), ((0,), (0,))
        ).astype(BF16)


def hidden_kernel(
    h1, h2, wo, x1, x2, gain, router, routes1, routes2,
    slots, hid, share_w,
    h2r, rs_send, rs_recv, ag_send, ag_recv, xt, pick,
    hs, hr, as_, ar, bs, br, cs, cr, local,
):
    dp = lax.axis_index("dp")
    ex = lax.axis_index("expert")
    y = dp // 2
    core = lax.rem(dp, 2)
    greet((("dp", ND), ("expert", NE)))

    def h_copy(peer, slot):
        return rcopy(h2.at[peer], h2r.at[slot], hs.at[peer], hr.at[slot], "dp", peer)

    def h_start(k, carry):
        h_copy(lax.rem(dp + k, ND), dp).start()
        return carry

    def h_wait(k, carry):
        peer = lax.rem(dp + k, ND)
        h_copy(peer, peer).wait_recv()
        return carry

    def h_sent(k, carry):
        peer = lax.rem(dp + k, ND)
        h_copy(peer, peer).wait_send()
        return carry

    lax.fori_loop(1, ND, h_start, 0)

    order = iota((R1, R1), 0)
    source = jnp.where(order < 32, 2 * order, 2 * (order - 32) + 1)
    perm = (iota((R1, R1), 1) == source).astype(BF16)
    heads1 = dot(perm, h1[...]).astype(BF16)
    part1 = dot(heads1, wo[...])
    for ct in range(NCT):
        for rb in range(4):
            t = ct * 6 + rb
            rs_send[t // 4, t % 4] = part1[
                rb * 16 : rb * 16 + 16, ct * 128 : ct * 128 + 128
            ].astype(BF16)
    xp = dot(perm, x1[...]).astype(BF16)
    for ct in range(NCT):
        for rb in range(6):
            src = xp[rb * 16 : rb * 16 + 16, ct * 128 : ct * 128 + 128] if rb < 4 else x2[(rb - 4) * 16 : (rb - 4) * 16 + 16, ct * 128 : ct * 128 + 128]
            xt[ct * 6 + rb] = src

    lanes = iota((R1, 128), 1)
    tab1 = routes1[pl.ds(pl.multiple_of(dp * R1, R1), R1), :]
    tab2 = routes2[pl.ds(pl.multiple_of(dp * R2, R2), R2), :]

    def multi_hot(tab, rows):
        hot = jnp.zeros((rows, 128), F32)
        for k in range(8):
            hot = hot + (tab[:, k : k + 1] == lanes[0:rows]).astype(F32)
        return hot

    mask1 = dot(perm, multi_hot(tab1, R1).astype(BF16))
    mask2 = multi_hot(tab2, R2)
    tri = (iota((R1, R1), 0) >= iota((R1, R1), 1)).astype(BF16)
    rank1 = mask1 * dot(tri, mask1.astype(BF16))
    rank2 = mask2 * dot(tri[0:R2, 0:R2], mask2.astype(BF16))
    mask = jnp.concatenate([mask1, mask2], axis=0)
    rank = jnp.concatenate([rank1, rank2], axis=0).astype(BF16)

    def expert_of(s):
        return 4 * ex + jnp.where(s < 32, s >> 3, (s - 32) >> 2)

    def place_of(s):
        return jnp.where(s < 32, s & 7, (s - 32) & 3) + 1

    ex_a = (iota((128, SLOTS), 0) == expert_of(iota((128, SLOTS), 1))).astype(F32)
    ex_b = (iota((SLOTS, 128), 1) == expert_of(iota((SLOTS, 128), 0))).astype(BF16)
    place_a = place_of(iota((RT, SLOTS), 1)).astype(F32)
    place_b = place_of(iota((SLOTS, RT), 0)).astype(F32)
    kind_a = (iota((RT, SLOTS), 0) < R1) == (iota((RT, SLOTS), 1) < 32)
    kind_b = (iota((SLOTS, RT), 1) < R1) == (iota((SLOTS, RT), 0) < 32)
    sel_a = jnp.where(kind_a & (dot(rank, ex_a.astype(BF16)) == place_a), 1.0, 0.0)
    sel_b = jnp.where(kind_b & (dot(ex_b, rank, ((1,), (1,))) == place_b), 1.0, 0.0)

    lax.fori_loop(1, ND, h_wait, 0)
    h2r[dp] = h2[dp]
    heads2 = h2r[0].astype(F32)
    for g in range(1, ND):
        heads2 = heads2 + h2r[g].astype(F32)
    part2 = dot(heads2.astype(BF16), wo[...])
    for ct in range(NCT):
        for rb in range(2):
            t = ct * 6 + 4 + rb
            rs_send[t // 4, t % 4] = part2[
                rb * 16 : rb * 16 + 16, ct * 128 : ct * 128 + 128
            ].astype(BF16)

    def a_copy(peer, slot):
        return rcopy(rs_send.at[peer], rs_recv.at[slot], as_.at[peer], ar.at[slot], "expert", peer)

    def a_start(k, carry):
        peer = lax.rem(ex + k, NE)

        @pl.when(peer < NOWN)
        def _():
            a_copy(peer, ex).start()

        return carry

    def a_sent(k, carry):
        peer = lax.rem(ex + k, NE)

        @pl.when(peer < NOWN)
        def _():
            a_copy(peer, ex).wait_send()

        return carry

    def a_wait(k, carry):
        a_copy(lax.rem(ex + NE - k, NE), lax.rem(ex + NE - k, NE)).wait_recv()
        return carry

    def b_copy(peer, slot):
        return rcopy(ag_send, ag_recv.at[slot], bs.at[peer], br.at[slot], "expert", peer)

    def b_start(k, carry):
        b_copy(lax.rem(ex + k, NE), ex).start()
        return carry

    def b_sent(k, carry):
        b_copy(lax.rem(ex + k, NE), ex).wait_send()
        return carry

    def b_wait(k, carry):
        peer = lax.rem(ex + NE - k, NE)

        @pl.when(peer < NOWN)
        def _():
            b_copy(peer, peer).wait_recv()

        return carry

    lax.fori_loop(1, NE, a_start, 0)

    @pl.when(ex < NOWN)
    def _():
        rs_recv[ex] = rs_send[ex]
        lax.fori_loop(1, NE, a_wait, 0)

        def add(s, total):
            return total + rs_recv[s].astype(F32)

        total = lax.fori_loop(0, NE, add, jnp.zeros((4, 16, 128), F32))
        total = total + xt[pl.ds(4 * ex, 4)].astype(F32)
        ag_send[...] = total.astype(BF16)
        ag_recv[ex] = ag_send[...]
        lax.fori_loop(1, NE, b_start, 0)

    lax.fori_loop(1, NE, b_wait, 0)
    for ct in range(NCT):
        for rb in range(6):
            t = ct * 6 + rb
            hid[rb * 16 : rb * 16 + 16, ct * 128 : ct * 128 + 128] = ag_recv[t // 4, t % 4]
    normed = rms(hid[...].astype(F32), gain[...]).astype(BF16)
    pick[...] = dot(sel_b.astype(BF16), normed).astype(BF16)

    def c_copy(src, slot, peer, sem):
        return rcopy(src, slots.at[slot], cs.at[sem], cr.at[slot], "dp", peer)

    def same(s):
        return 2 * lax.rem(y + s, 4) + core

    def sib(s):
        return 2 * lax.rem(y + s, 4) + 1 - core

    sibling = sib(0)
    for s in (2, 1, 3):
        c_copy(pick, dp, same(s), s).start()
    c_copy(pick, dp, sibling, 0).start()
    own = pltpu.make_async_copy(pick, slots.at[dp], local)
    own.start()

    logits = dot(normed, router[...])
    scores = jax.nn.sigmoid(logits) * mask
    shares = ROUTE_SCALE * scores / jnp.sum(scores, axis=-1, keepdims=True)
    share_w[...] = dot(shares, ex_a, precision=lax.Precision.HIGHEST) * sel_a

    for s in (1, 3, 2):
        c_copy(pick, same(s), same(s), s).wait_recv()
        c_copy(slots.at[same(s)], same(s), sibling, 3 + s).start()
    own.wait()
    for s in (0, 1, 3, 2):
        c_copy(pick, sib(s), sibling, 0).wait_recv()
    for s in (0, 1, 2, 3):
        c_copy(pick, dp, sibling, s).wait_send()
    for s in (1, 2, 3):
        c_copy(slots.at[same(s)], same(s), sibling, 3 + s).wait_send()
    lax.fori_loop(1, ND, h_sent, 0)
    lax.fori_loop(1, NE, a_sent, 0)

    @pl.when(ex < NOWN)
    def _():
        lax.fori_loop(1, NE, b_sent, 0)


def expert_kernel(slots, wg, wu, wd, out, acc):
    e = pl.program_id(0)
    pair = e // 2

    @pl.when(e == 0)
    def _():
        acc[...] = jnp.zeros_like(acc)

    def apply(rows, mine):
        x = slots[:, rows, :].reshape(ND * 16, D)
        g = dot(x, wg[0])
        u = dot(x, wu[0])
        active = g * jax.nn.sigmoid(g) * u
        place = iota((ND * 16, H), 0) & 15
        active = jnp.where(mine(place), active, 0.0).astype(BF16)
        acc[:, rows, :] += dot(active, wd[0]).reshape(ND, 16, D)

    apply(pl.ds(pl.multiple_of(16 * pair, 16), 16), lambda p: (p >> 3) == e - 2 * pair)
    apply(pl.ds(32, 16), lambda p: (p >> 2) == e)

    @pl.when(e == pl.num_programs(0) - 1)
    def _():
        out[...] = acc[...].astype(BF16)


def combine_kernel(
    out, hid, share_w, first, tail,
    pr, z, zr, scr, e_send, e_recv, rows,
    ps, prs, zs, zrs, es, er,
):
    dp = lax.axis_index("dp")
    ex = lax.axis_index("expert")
    y = dp // 2
    core = lax.rem(dp, 2)
    greet((("dp", ND), ("expert", NE)))

    def p_copy(yy):
        return rcopy(out.at[2 * yy + 1 - core], pr.at[yy], ps.at[yy], prs.at[yy], "dp", 2 * y + 1 - core)

    def z_copy(s, slot):
        yy = lax.rem(y + s, 4)
        return rcopy(z.at[yy], zr.at[slot], zs.at[yy], zrs.at[slot], "dp", 2 * yy + core)

    for s in (2, 1, 3, 0):
        p_copy(lax.rem(y + s, 4)).start()
    for s in (2, 1, 3):
        yy = lax.rem(y + s, 4)
        p_copy(yy).wait_recv()
        z[yy] = (out[2 * yy + core].astype(F32) + pr[yy].astype(F32)).astype(BF16)
        z_copy(s, y).start()
    p_copy(y).wait_recv()
    total = out[dp].astype(F32) + pr[y].astype(F32)
    for s in (1, 3, 2):
        yy = lax.rem(y + s, 4)
        z_copy(s, yy).wait_recv()
        total = total + zr[yy].astype(F32)
    summed = total.astype(BF16)
    w = share_w[...]
    w_hi = w.astype(BF16)
    w_lo = (w - w_hi.astype(F32)).astype(BF16)
    r = iota((RT, RT), 0)
    mine = ((r == iota((RT, RT), 1)) & ((r & 31) == ex)).astype(BF16)
    res = dot(w_hi, summed) + dot(w_lo, summed) + dot(mine, hid[...])
    for ct in range(NCT):
        for j in range(3):
            scr[pl.ds(j * NCT + ct, NE, stride=64), :] = res[
                j * 32 : j * 32 + 32, ct * 128 : ct * 128 + 128
            ]
    for c in range(NE):
        e_send[c] = scr[c * 64 : c * 64 + 64, :].astype(BF16)

    def e_copy(peer, slot):
        return rcopy(e_send.at[peer], e_recv.at[slot], es.at[peer], er.at[slot], "expert", peer)

    def e_start(k, carry):
        e_copy(lax.rem(ex + k, NE), ex).start()
        return carry

    def e_wait(k, carry):
        peer = lax.rem(ex + NE - k, NE)
        e_copy(peer, peer).wait_recv()
        return carry

    def e_sent(k, carry):
        e_copy(lax.rem(ex + k, NE), ex).wait_send()
        return carry

    lax.fori_loop(1, NE, e_start, 0)
    e_recv[ex] = jnp.zeros((64, 128), BF16)
    lax.fori_loop(1, NE, e_wait, 0)

    def add(s, total):
        return total + e_recv[s].astype(F32)

    total = scr[pl.ds(pl.multiple_of(ex * 64, 64), 64), :]
    total = lax.fori_loop(0, NE, add, total)
    for j in range(3):
        for ct in range(NCT):
            at = j * NCT + ct
            rows[j : j + 1, ct * 128 : ct * 128 + 128] = total[at : at + 1, :]
    first[...] = rows[0:2, :].astype(BF16)
    tail[...] = rows[2:3, :].astype(BF16)
    lax.fori_loop(1, NE, e_sent, 0)
    for s in (0, 1, 2, 3):
        p_copy(lax.rem(y + s, 4)).wait_send()
    for s in (1, 2, 3):
        z_copy(s, y).wait_send()


def params(collective_id=None):
    if collective_id is None:
        return pltpu.CompilerParams(vmem_limit_bytes=VMEM_LIMIT)
    return pltpu.CompilerParams(
        vmem_limit_bytes=VMEM_LIMIT, collective_id=collective_id, has_side_effects=True
    )


VM = pl.BlockSpec(memory_space=pltpu.VMEM)
SM = pl.BlockSpec(memory_space=pltpu.SMEM)
DMA = pltpu.SemaphoreType.DMA


def shape(dims, dtype):
    return jax.ShapeDtypeStruct(dims, dtype)


def on_device(
    inputs, tail_inputs, states, tail_ids, routes, tail_routes, attention_gain,
    query_weight, key_weight, value_weight, decay_down, decay_up, decay_bias,
    decay_log, beta_weight, output_gain, head_out, expert_gain, router_weight,
    gate_weight, up_weight, down_weight,
):
    p1, p2 = pl.pallas_call(
        project_kernel,
        out_shape=(shape((R1, 8 * H), F32), shape((R2, 4 * H), BF16)),
        in_specs=[VM] * 9 + [SM, VM],
        out_specs=(VM, VM),
        scratch_shapes=[pltpu.VMEM((RT, D), BF16)],
        compiler_params=params(),
        name="project",
    )(
        inputs, tail_inputs, attention_gain.reshape(1, D), query_weight, key_weight,
        value_weight, decay_down, decay_up, decay_bias.reshape(1, H), decay_log,
        beta_weight.reshape(1, D),
    )
    p2all = pl.pallas_call(
        share_kernel,
        out_shape=shape((ND, R2, 4 * H), BF16),
        in_specs=[VM],
        out_specs=VM,
        scratch_shapes=[DMA((ND,)), DMA((ND,)), DMA],
        compiler_params=params(0),
        name="share_rows",
    )(p2)
    h1, h2 = pl.pallas_call(
        attend_kernel,
        grid=(8,),
        out_shape=(shape((R1, H), BF16), shape((ND * R2, H), BF16)),
        in_specs=[
            pl.BlockSpec((8, 8 * H), lambda i: (i, 0)),
            pl.BlockSpec((ND * R2, 4 * H), lambda i: (0, 0)),
            pl.BlockSpec((8, H, H), lambda i: (i, 0, 0)),
            pl.BlockSpec((1, 256), lambda i: (0, 0)),
            pl.BlockSpec((1, H), lambda i: (0, 0)),
        ],
        out_specs=(
            pl.BlockSpec((R1, H), lambda i: (0, 0)),
            pl.BlockSpec((ND * R2, H), lambda i: (0, 0)),
        ),
        scratch_shapes=[
            pltpu.VMEM((R1, 256), F32),
            pltpu.VMEM((R1, 4 * H), F32),
            pltpu.VMEM((R1, H), F32),
            pltpu.VMEM((R1, H), F32),
            pltpu.VMEM((8, H), F32),
            pltpu.VMEM((8, H), F32),
        ],
        compiler_params=params(),
        name="attend",
    )(
        p1, p2all.reshape(ND * R2, 4 * H), states.reshape(R1, H, H),
        tail_ids.reshape(1, 256), output_gain.reshape(1, H),
    )
    slots, hid, share_w = pl.pallas_call(
        hidden_kernel,
        out_shape=(
            shape((ND, SLOTS, D), BF16),
            shape((RT, D), BF16),
            shape((RT, SLOTS), F32),
        ),
        in_specs=[VM] * 9,
        out_specs=(VM, VM, VM),
        scratch_shapes=[
            pltpu.VMEM((ND, R2, H), BF16),
            pltpu.VMEM((NE, 4, 16, 128), BF16),
            pltpu.VMEM((NE, 4, 16, 128), BF16),
            pltpu.VMEM((4, 16, 128), BF16),
            pltpu.VMEM((NE, 4, 16, 128), BF16),
            pltpu.VMEM((NE * 4, 16, 128), BF16),
            pltpu.VMEM((SLOTS, D), BF16),
            DMA((ND,)), DMA((ND,)),
            DMA((NE,)), DMA((NE,)),
            DMA((NE,)), DMA((NE,)),
            DMA((ND,)), DMA((ND,)),
            DMA,
        ],
        compiler_params=params(1),
        name="hidden",
    )(
        h1, h2.reshape(ND, R2, H), head_out, inputs, tail_inputs,
        expert_gain.reshape(1, D), router_weight, routes, tail_routes,
    )
    out = pl.pallas_call(
        expert_kernel,
        grid=(4,),
        out_shape=shape((ND, SLOTS, D), BF16),
        in_specs=[
            pl.BlockSpec((ND, SLOTS, D), lambda e: (0, 0, 0)),
            pl.BlockSpec((1, D, H), lambda e: (e, 0, 0)),
            pl.BlockSpec((1, D, H), lambda e: (e, 0, 0)),
            pl.BlockSpec((1, H, D), lambda e: (e, 0, 0)),
        ],
        out_specs=pl.BlockSpec((ND, SLOTS, D), lambda e: (0, 0, 0)),
        scratch_shapes=[pltpu.VMEM((ND, SLOTS, D), F32)],
        compiler_params=params(),
        name="experts",
    )(slots, gate_weight, up_weight, down_weight)
    return pl.pallas_call(
        combine_kernel,
        out_shape=(shape((2, D), BF16), shape((1, D), BF16)),
        in_specs=[VM] * 3,
        out_specs=(VM, VM),
        scratch_shapes=[
            pltpu.VMEM((4, SLOTS, D), BF16),
            pltpu.VMEM((4, SLOTS, D), BF16),
            pltpu.VMEM((4, SLOTS, D), BF16),
            pltpu.VMEM((NE * 64, 128), F32),
            pltpu.VMEM((NE, 64, 128), BF16),
            pltpu.VMEM((NE, 64, 128), BF16),
            pltpu.VMEM((8, D), F32),
            DMA((4,)), DMA((4,)),
            DMA((4,)), DMA((4,)),
            DMA((NE,)), DMA((NE,)),
        ],
        compiler_params=params(2),
        name="combine",
    )(out, hid, share_w)


def solution(mesh):
    placed = (
        P("dp", None),
        P("dp", None),
        P("dp", "expert", None, None),
        P(),
        P(),
        P(),
        P(),
        P(None, "expert"),
        P(None, "expert"),
        P(None, "expert"),
        P(),
        P(None, "expert"),
        P("expert"),
        P("expert"),
        P(None, "expert"),
        P(),
        P("expert", None),
        P(),
        P(),
        P("expert", None, "dp"),
        P("expert", None, "dp"),
        P("expert", "dp", None),
    )
    return jax.shard_map(
        on_device,
        mesh=mesh,
        in_specs=placed,
        out_specs=(P(("dp", "expert"), None), P(("dp", "expert"), None)),
        check_vma=False,
    )
```

```python
import jax
import jax.numpy as jnp
from jax import lax
from jax.experimental import pallas as pl
from jax.experimental.pallas import tpu as pltpu
from jax.sharding import PartitionSpec as P

F32 = jnp.float32
BF16 = jnp.bfloat16
EPS = 1e-06
ROUTE_SCALE = 2.446
MESH = pl.DeviceIdType.MESH
VMEM_LIMIT = 56 * 1024 * 1024
D = 2304
H = 128
NCT = D // 128
R1 = 64
R2 = 32
RT = R1 + R2
ND = 8
NX = 4
NZ = 8
ROWS = (64, 32)
SLOTS = (32, 16)
TILES = (18, 9)
OWNERS = (6, 3)
OUTS = (48, 32)
AX, AZ, BZ, BX, CC, DP, DY, EX, EZ = range(0, 18, 2)
KINDS = 18
PACK, HEAD = 2 * KINDS, 2 * KINDS + 2
SEM_ROWS = 2 * KINDS + 4


def iota(shape, dim):
    return lax.broadcasted_iota(jnp.int32, shape, dim)


def dot(a, b, contract=((1,), (0,)), precision=None):
    return lax.dot_general(
        a, b, (contract, ((), ())), precision=precision, preferred_element_type=F32
    )


def rms(wide, gain):
    factor = lax.rsqrt(jnp.mean(wide * wide, axis=-1, keepdims=True) + EPS)
    return wide * factor * gain


def cols(c):
    return slice(c * 128, c * 128 + 128)


def each(lo, hi, body):
    def step(k, carry):
        body(k)
        return carry

    lax.fori_loop(lo, hi, step, 0)


def kernel(
    x1h, x2h, sth, wqh, wkh, wvh, wddh, wduh, woh, roh, wgh, wuh, wdh,
    again, bias, dlog, wb, og, egain, ids, routes1, routes2,
    first, tail,
    x1, x2, st, wq, wk, wv, wdd, wdu, wo, ro, wg, wu, wd,
    lsem, ssem, sem,
    normed, p1, p2all, named, tp, fresh, h1s, h2s, blk, h2c, h2r,
    ax_s1, ax_s2, ax_r1, ax_r2, az_s1, az_s2, az_r1, az_r2,
    rt1, rt2, hb1, hb2, hid1, hid2,
    slots1, slots2, out1, out2, pr1, pr2, zb1, zb2, zr1, zr2,
    ex_s1, ex_s2, ex_r1, ex_r2, res1, res2,
    scr1, scr2, ez_s1, ez_s2, ez_r1, ez_r2, rows,
):
    ax_s, ax_r, az_s, az_r = (ax_s1, ax_s2), (ax_r1, ax_r2), (az_s1, az_s2), (az_r1, az_r2)
    rt, hb, hid = (rt1, rt2), (hb1, hb2), (hid1, hid2)
    slots, out, pr, zb, zr = (slots1, slots2), (out1, out2), (pr1, pr2), (zb1, zb2), (zr1, zr2)
    ex_s, ex_r, res, scr = (ex_s1, ex_s2), (ex_r1, ex_r2), (res1, res2), (scr1, scr2)
    ez_s, ez_r = (ez_s1, ez_s2), (ez_r1, ez_r2)
    dp = lax.axis_index("dp")
    ex = lax.axis_index("expert")
    y = dp // 2
    core = lax.rem(dp, 2)
    xx = ex // NZ
    z = lax.rem(ex, NZ)

    def same(s):
        return 2 * lax.rem(y + s, 4) + core

    def other(s):
        return 2 * lax.rem(y + s, 4) + 1 - core

    def xat(s):
        return lax.rem(xx + s, NX)

    def zat(s):
        return lax.rem(z + s, NZ)

    def xdev(s):
        return {"expert": xat(s) * NZ + z}

    def zdev(s):
        return {"expert": xx * NZ + zat(s)}

    def rcopy(src, dst, row, snd, rcv, device):
        return pltpu.make_async_remote_copy(
            src_ref=src,
            dst_ref=dst,
            send_sem=sem.at[row, snd],
            recv_sem=sem.at[row + 1, rcv],
            device_id=device,
            device_id_type=MESH,
        )

    loads = []
    for n, (src, dst) in enumerate(
        (
            (x2h, x2), (x1h, x1), (wqh, wq), (wkh, wk), (wvh, wv), (wddh, wdd), (wduh, wdu),
        )
    ):
        loads.append(pltpu.make_async_copy(src, dst, lsem.at[n]))

    def load_state(i):
        part = pl.ds(i * 8, 8)
        return pltpu.make_async_copy(sth.at[part], st.at[part], ssem.at[i])

    later = []
    for n, (src, dst) in enumerate(((woh, wo), (roh, ro), (wgh, wg), (wuh, wu), (wdh, wd))):
        later.append(pltpu.make_async_copy(src, dst, lsem.at[7 + n]))
    for copy in loads:
        copy.start()
    barrier = pltpu.get_barrier_semaphore()
    for s in range(1, ND):
        pl.semaphore_signal(barrier, inc=1, device_id={"dp": lax.rem(dp + s, ND)}, device_id_type=MESH)
    for s in range(1, NX):
        pl.semaphore_signal(barrier, inc=1, device_id=xdev(s), device_id_type=MESH)
    for s in range(1, NZ):
        pl.semaphore_signal(barrier, inc=1, device_id=zdev(s), device_id_type=MESH)
    each(0, 8, lambda i: load_state(i).start())
    for copy in later:
        copy.start()
    load_wo, load_ro = later[0], later[1]

    for copy in loads:
        copy.wait()
    normed[0:R1, :] = rms(x1[...].astype(F32), again[...]).astype(BF16)
    normed[R1:RT, :] = rms(x2[...].astype(F32), again[...]).astype(BF16)
    n = normed[...]

    def project(w):
        produced = dot(n, w[...])
        return produced * jax.nn.sigmoid(produced)

    def unit(v):
        return v * lax.rsqrt(jnp.sum(v * v, axis=-1, keepdims=True) + EPS)

    q = unit(project(wq))
    k = unit(project(wk))
    v = project(wv)
    low = dot(n, wdd[...]).astype(BF16)
    gate = dot(low, wdu[...]) + bias[...]
    soft = jnp.maximum(gate, 0.0) + jnp.log(1.0 + jnp.exp(-jnp.abs(gate)))
    strength = jnp.exp(jnp.full((RT, H), dlog[0], F32))
    decay = jnp.exp(-(strength * soft))
    beta = jax.nn.sigmoid(
        jnp.sum(n.astype(F32) * wb[...].astype(F32), axis=-1, keepdims=True)
    )
    dk = decay * k
    dq = decay * q
    sc = jnp.broadcast_to(beta * jnp.sum(k * q, axis=-1, keepdims=True), (RT, H))
    for c, part in enumerate((dk, dq, v, sc)):
        p2all[dp, :, cols(c)] = part[R1:RT, :].astype(BF16)
    pl.semaphore_wait(barrier, ND + NX + NZ - 3)

    def pack_copy(s, slot):
        return rcopy(
            p2all.at[dp], p2all.at[slot], PACK, s, slot, {"dp": lax.rem(dp + s, ND)}
        )

    each(1, ND, lambda s: pack_copy(s, dp).start())
    dk_hi = dk.astype(BF16).astype(F32)
    dq_hi = dq.astype(BF16).astype(F32)
    parts = (dk_hi, dk - dk_hi, dq_hi, dq - dq_hi, v, sc, decay, beta * k)
    for c, part in enumerate(parts):
        p1[:, cols(c)] = part[0:R1, :]

    m = iota((16, H), 0)

    def first_block(i):
        load_state(i).wait()
        at = pl.ds(pl.multiple_of(i * 8, 8), 8)
        t = p1[at, :]
        dcol = jnp.transpose(t[:, cols(6)])
        bcol = jnp.transpose(t[:, cols(7)])
        for j in range(8):
            row = [t[j : j + 1, cols(c)] for c in range(6)]
            state = st[i * 8 + j]
            a = jnp.where(m == 0, row[0], jnp.where(m == 1, row[1], jnp.where(m == 2, row[2], row[3])))
            got = dot(a.astype(BF16), state)
            u = row[4] - (got[0:1] + got[1:2])
            blk[j : j + 1, :] = got[2:3] + got[3:4] + row[5] * u
            fresh[i * 8 + j] = (
                state.astype(F32) * dcol[:, j : j + 1] + bcol[:, j : j + 1] * u
            ).astype(BF16)
        h1s[at, :] = rms(blk[...] * H**-0.5, og[...])

    each(0, 8, first_block)

    order = iota((R1, R1), 0)
    within = order & 15
    source = order - within + jnp.where(within < 8, 2 * within, 2 * (within - 8) + 1)
    perm = (iota((R1, R1), 1) == source).astype(BF16)

    def tile(p, val, xi, c):
        if p == 0:
            return val[xi * 16 : xi * 16 + 16, cols(c)]
        return jnp.concatenate(
            [val[xi * 8 : xi * 8 + 8, cols(2 * c)], val[xi * 8 : xi * 8 + 8, cols(2 * c + 1)]], axis=0
        )

    def a_send(p, val):
        for xi in range(NX):
            for c in range(TILES[p]):
                ax_s[p][xi, c] = tile(p, val, xi, c).astype(BF16)
        for s in (2, 1, 3):
            ax_copy(p, s, xx).start()

    def ax_copy(p, s, slot):
        return rcopy(ax_s[p].at[xat(s)], ax_r[p].at[slot], AX + KINDS * p, s, slot, xdev(s))

    def az_copy(p, s, slot):
        return rcopy(
            az_s[p].at[pl.ds(3 * zat(s), 3)], az_r[p].at[slot], AZ + KINDS * p, s, slot, zdev(s)
        )

    def az_own(p, slot):
        return rcopy(
            az_s[p].at[pl.ds(0, 3)], az_r[p].at[slot], AZ + KINDS * p, 0, slot, zdev(0)
        )

    def bz_copy(p, s, owner):
        part = hb[p].at[xx, pl.ds(3 * owner, 3)]
        return rcopy(part, part, BZ + KINDS * p, s, owner, zdev(s))

    def bx_copy(p, s, owner):
        part = hb[p].at[owner]
        return rcopy(part, part, BX + KINDS * p, s, owner, xdev(s))

    def a_turn(p):
        total = ax_s[p][xx].astype(F32)
        for s in (1, 3, 2):
            ax_copy(p, s, xat(s)).wait_recv()
            total = total + ax_r[p][xat(s)].astype(F32)
        az_s[p][...] = total.astype(BF16)
        for s in (4, 3, 5, 2, 6, 1, 7):

            @pl.when(zat(s) < OWNERS[p])
            def _():
                az_copy(p, s, z).start()

    def b_start(p):
        @pl.when(z < OWNERS[p])
        def _():
            mine = pl.ds(3 * z, 3)
            total = az_s[p][mine].astype(F32) + rt[p][xx, mine].astype(F32)
            for s in (1, 7, 2, 6, 3, 5, 4):
                az_own(p, zat(s)).wait_recv()
                total = total + az_r[p][zat(s)].astype(F32)
            hb[p][xx, mine] = total.astype(BF16)
            for s in (4, 3, 5, 2, 6, 1, 7):
                bz_copy(p, s, z).start()

    def b_turn(p):
        for s in (1, 7, 2, 6, 3, 5, 4):

            @pl.when(zat(s) < OWNERS[p])
            def _():
                bz_copy(p, s, zat(s)).wait_recv()

        for s in (2, 1, 3):
            bx_copy(p, s, xx).start()

    def b_end(p):
        for s in (1, 3, 2):
            bx_copy(p, s, xat(s)).wait_recv()
        for xi in range(NX):
            for c in range(TILES[p]):
                got = hb[p][xi, c].astype(F32)
                if p == 0:
                    hid1[xi * 16 : xi * 16 + 16, cols(c)] = got
                else:
                    hid2[xi * 8 : xi * 8 + 8, cols(2 * c)] = got[0:8]
                    hid2[xi * 8 : xi * 8 + 8, cols(2 * c + 1)] = got[8:16]

    load_wo.wait()
    a_send(0, dot(dot(perm, h1s[...].astype(BF16)).astype(BF16), wo[...]))

    base = dp * R1
    named[...] = (ids[...] == base + iota((R1, 256), 0)).astype(F32)
    for s in range(1, ND):
        pack_copy(s, lax.rem(dp + s, ND)).wait_recv()
    tp[...] = dot(named[...].astype(BF16), p2all[...].reshape(ND * R2, 4 * H))

    def second_block(i):
        at = pl.ds(pl.multiple_of(i * 8, 8), 8)
        t = tp[at, :]
        for j in range(8):
            row = [t[j : j + 1, cols(c)] for c in range(4)]
            a = jnp.where(m == 0, row[0], row[1])
            got = dot(a.astype(BF16), fresh[i * 8 + j])
            blk[j : j + 1, :] = got[1:2] + row[3] * (row[2] - got[0:1])
        h2s[at, :] = rms(blk[...] * H**-0.5, og[...])

    each(0, 8, second_block)
    h2c[...] = dot(named[...].astype(BF16), h2s[...].astype(BF16), ((0,), (0,))).astype(
        BF16
    ).reshape(ND, R2, H)

    def head_copy(s, slot):
        peer = lax.rem(dp + s, ND)
        return rcopy(h2c.at[peer], h2r.at[slot], HEAD, s, slot, {"dp": peer})

    each(1, ND, lambda s: head_copy(s, dp).start())

    xp = dot(perm, x1[...])
    x2v = x2[...].astype(F32)
    for xi in range(NX):
        for c in range(TILES[0]):
            rt1[xi, c] = tile(0, xp, xi, c).astype(BF16)
        for c in range(TILES[1]):
            rt2[xi, c] = tile(1, x2v, xi, c).astype(BF16)
    a_turn(0)

    def multi_hot(tab, count):
        hot = jnp.zeros((count, 128), F32)
        for c in range(8):
            hot = hot + (tab[:, c : c + 1] == iota((count, 128), 1)).astype(F32)
        return hot

    tab1 = routes1[pl.ds(pl.multiple_of(dp * R1, R1), R1), :]
    tab2 = routes2[pl.ds(pl.multiple_of(dp * R2, R2), R2), :]
    mask = (dot(perm, multi_hot(tab1, R1).astype(BF16)), multi_hot(tab2, R2))
    expert_a, select, place = [], [], []
    for p in range(2):
        r, n_slots, cap = ROWS[p], SLOTS[p], (3, 2)[p]
        tri = (iota((r, r), 0) >= iota((r, r), 1)).astype(BF16)
        rank = (mask[p] * dot(tri, mask[p].astype(BF16))).astype(BF16)
        sa, sb = iota((128, n_slots), 1), iota((n_slots, 128), 0)
        hot_a = iota((128, n_slots), 0) == 4 * ex + (sa >> cap)
        hot_b = iota((n_slots, 128), 1) == 4 * ex + (sb >> cap)
        at_a = (iota((r, n_slots), 1) & ((1 << cap) - 1)) + 1
        at_b = (iota((n_slots, r), 0) & ((1 << cap) - 1)) + 1
        expert_a.append(hot_a.astype(F32))
        place.append((dot(rank, hot_a.astype(BF16)) == at_a.astype(F32)).astype(F32))
        select.append((dot(hot_b.astype(BF16), rank, ((1,), (1,))) == at_b.astype(F32)).astype(BF16))

    for s in range(1, ND):
        head_copy(s, lax.rem(dp + s, ND)).wait_recv()
    h2r[dp] = h2c[dp]
    heads2 = h2r[0].astype(F32)
    for g in range(1, ND):
        heads2 = heads2 + h2r[g].astype(F32)
    a_send(1, dot(heads2.astype(BF16), wo[...]))
    b_start(0)
    a_turn(1)
    b_turn(0)
    b_start(1)

    def c_copy(p, slot, row, device):
        part = slots[p].at[slot]
        return rcopy(part, part, CC + KINDS * p, row, slot, {"dp": device})

    def c_start(p):
        normed_p = rms(hid[p][...], egain[...]).astype(BF16)
        slots[p][dp] = dot(select[p], normed_p).astype(BF16)
        for s in (2, 1, 3):
            c_copy(p, dp, s, same(s)).start()
        c_copy(p, dp, 0, other(0)).start()
        return normed_p

    def c_turn(p):
        for s in (1, 3, 2):
            c_copy(p, same(s), s, same(s)).wait_recv()
            c_copy(p, same(s), 3 + s, other(0)).start()

    def c_end(p):
        for s in (0, 1, 3, 2):
            c_copy(p, other(s), 0, other(0)).wait_recv()

    def weights(p, normed_p):
        scores = jax.nn.sigmoid(dot(normed_p, ro[...])) * mask[p]
        shares = ROUTE_SCALE * scores / jnp.sum(scores, axis=-1, keepdims=True)
        return dot(shares, expert_a[p], precision=lax.Precision.HIGHEST) * place[p]

    b_end(0)
    n0 = c_start(0)
    b_turn(1)
    load_ro.wait()
    w0 = weights(0, n0)
    b_end(1)
    n1 = c_start(1)
    w1 = weights(1, n1)
    share = (w0, w1)
    for copy in later[2:]:
        copy.wait()

    def hidden_units(x, e, mine):
        g = dot(x, wg[e])
        u = dot(x, wu[e])
        return jnp.where(mine, g * jax.nn.sigmoid(g) * u, 0.0).astype(BF16)

    spot = iota((ND * 16, H), 0) & 15

    def experts(p):
        if p == 0:
            for pair in range(2):
                x = slots1[:, 16 * pair : 16 * pair + 16, :].reshape(ND * 16, D)
                a0 = hidden_units(x, 2 * pair, (spot >> 3) == 0)
                a1 = hidden_units(x, 2 * pair + 1, (spot >> 3) == 1)
                for c in range(0, D, 768):
                    cc = slice(c, c + 768)
                    got = dot(a0, wd[2 * pair, :, cc]) + dot(a1, wd[2 * pair + 1, :, cc])
                    out1[:, 16 * pair : 16 * pair + 16, cc] = got.astype(BF16).reshape(ND, 16, 768)
        else:
            x = slots2[...].reshape(ND * 16, D)
            acts = [hidden_units(x, e, (spot >> 2) == e) for e in range(4)]
            for c in range(0, D, 768):
                cc = slice(c, c + 768)
                got = dot(acts[0], wd[0, :, cc])
                for e in range(1, 4):
                    got = got + dot(acts[e], wd[e, :, cc])
                out2[:, :, cc] = got.astype(BF16).reshape(ND, 16, 768)

    def pair_copy(p, s):
        yy = lax.rem(y + s, 4)
        return rcopy(out[p].at[other(s)], pr[p].at[yy], DP + KINDS * p, yy, yy, {"dp": other(0)})

    def chip_copy(p, s, slot):
        yy = lax.rem(y + s, 4)
        return rcopy(zb[p].at[yy], zr[p].at[slot], DY + KINDS * p, yy, slot, {"dp": same(s)})

    def d_start(p):
        for s in (2, 1, 3, 0):
            pair_copy(p, s).start()

    def d_turn(p):
        for s in (2, 1, 3):
            yy = lax.rem(y + s, 4)
            pair_copy(p, s).wait_recv()
            zb[p][yy] = (out[p][same(s)].astype(F32) + pr[p][yy].astype(F32)).astype(BF16)
            chip_copy(p, s, y).start()
        pair_copy(p, 0).wait_recv()

    def ex_copy(p, s, slot):
        return rcopy(ex_s[p].at[xat(s)], ex_r[p].at[slot], EX + KINDS * p, s, slot, xdev(s))

    def ez_copy(p, s, slot):
        return rcopy(ez_s[p].at[zat(s)], ez_r[p].at[slot], EZ + KINDS * p, s, slot, zdev(s))

    def e_start(p):
        total = out[p][dp].astype(F32) + pr[p][y].astype(F32)
        for s in (1, 3, 2):
            yy = lax.rem(y + s, 4)
            chip_copy(p, s, yy).wait_recv()
            total = total + zr[p][yy].astype(F32)
        summed = total.astype(BF16)
        w_hi = share[p].astype(BF16)
        w_lo = (share[p] - w_hi.astype(F32)).astype(BF16)
        got = dot(w_hi, summed) + dot(w_lo, summed)
        res[p][...] = got
        for xi in range(NX):
            for c in range(TILES[p]):
                ex_s[p][xi, c] = tile(p, got, xi, c).astype(BF16)
        for s in (2, 1, 3):
            ex_copy(p, s, xx).start()

    def e_turn(p):
        block = (16, 8)[p]
        at = pl.ds(pl.multiple_of(xx * block, block), block)
        own = (iota((block, 128), 0) & 7) == z
        for s in (1, 3, 2):
            ex_copy(p, s, xat(s)).wait_recv()
        scr[p][...] = jnp.zeros_like(scr[p])
        for c in range(TILES[p]):
            arrived = ex_r[p][xat(1), c].astype(F32)
            for s in (2, 3):
                arrived = arrived + ex_r[p][xat(s), c].astype(F32)
            for half in range(2):
                ct = c if p == 0 else 2 * c + half
                if p == 0 and half == 1:
                    continue
                mine = res[p][at, cols(ct)] + jnp.where(own, hid[p][at, cols(ct)], 0.0)
                if p == 0:
                    val = mine + arrived
                    scr1[pl.ds(ct, NZ, stride=48), :] = val[0:8]
                    scr1[pl.ds(NCT + ct, NZ, stride=48), :] = val[8:16]
                else:
                    scr2[pl.ds(ct, NZ, stride=32), :] = mine + arrived[8 * half : 8 * half + 8]
        w = OUTS[p]
        for zi in range(NZ):
            ez_s[p][zi] = scr[p][zi * w : zi * w + w, :].astype(BF16)
        for s in (4, 3, 5, 2, 6, 1, 7):
            ez_copy(p, s, z).start()

    def e_end(p):
        w = OUTS[p]
        total = scr[p][pl.ds(pl.multiple_of(z * w, w), w), :]
        for s in (1, 7, 2, 6, 3, 5, 4):
            ez_copy(p, s, zat(s)).wait_recv()
            total = total + ez_r[p][zat(s)].astype(F32)
        for j in range(2 - p):
            for ct in range(NCT):
                rows[2 * p + j : 2 * p + j + 1, cols(ct)] = total[j * NCT + ct : j * NCT + ct + 1, :]

    c_turn(0)
    c_end(0)
    experts(0)
    d_start(0)
    c_turn(1)
    d_turn(0)
    c_end(1)
    experts(1)
    d_start(1)
    d_turn(1)
    e_start(0)
    e_start(1)
    e_turn(0)
    e_turn(1)
    e_end(0)
    e_end(1)
    first[...] = rows[0:2, :].astype(BF16)
    tail[...] = rows[2:3, :].astype(BF16)

    each(1, ND, lambda s: pack_copy(s, dp).wait_send())
    each(1, ND, lambda s: head_copy(s, dp).wait_send())
    for p in range(2):
        for s in range(1, NX):
            ax_copy(p, s, xx).wait_send()
            bx_copy(p, s, xx).wait_send()
            ex_copy(p, s, xx).wait_send()
            chip_copy(p, s, y).wait_send()
            c_copy(p, dp, s, same(s)).wait_send()
            c_copy(p, same(s), 3 + s, other(0)).wait_send()
        for s in range(4):
            pair_copy(p, s).wait_send()
        c_copy(p, dp, 0, other(0)).wait_send()
        for s in range(1, NZ):
            ez_copy(p, s, z).wait_send()

            @pl.when(zat(s) < OWNERS[p])
            def _():
                az_copy(p, s, z).wait_send()

        @pl.when(z < OWNERS[p])
        def _():
            for s in range(1, NZ):
                bz_copy(p, s, z).wait_send()


VM = pl.BlockSpec(memory_space=pltpu.VMEM)
SM = pl.BlockSpec(memory_space=pltpu.SMEM)
HB = pl.BlockSpec(memory_space=pl.ANY)
DMA = pltpu.SemaphoreType.DMA


def on_device(
    inputs, tail_inputs, states, tail_ids, routes, tail_routes, attention_gain,
    query_weight, key_weight, value_weight, decay_down, decay_up, decay_bias,
    decay_log, beta_weight, output_gain, head_out, expert_gain, router_weight,
    gate_weight, up_weight, down_weight,
):
    def vm(*dims, dtype=BF16):
        return pltpu.VMEM(dims, dtype)

    def both(lead, rest, sizes, dtype=BF16):
        return [vm(*lead, n, *rest, dtype=dtype) for n in sizes]

    heavy = (
        inputs, tail_inputs, states.reshape(R1, H, H), query_weight, key_weight,
        value_weight, decay_down, decay_up, head_out, router_weight, gate_weight,
        up_weight, down_weight,
    )
    scratch = [vm(*a.shape) for a in heavy]
    scratch += [DMA((12,)), DMA((8,)), DMA((SEM_ROWS, 8))]
    scratch += [
        vm(RT, D), vm(R1, 8 * H, dtype=F32), vm(ND, R2, 4 * H), vm(R1, 256, dtype=F32),
        vm(R1, 4 * H, dtype=F32), vm(R1, H, H), vm(R1, H, dtype=F32), vm(R1, H, dtype=F32),
        vm(8, H, dtype=F32), vm(ND, R2, H), vm(ND, R2, H),
    ]
    t = (16, 128)
    scratch += both((NX,), t, TILES) + both((NX,), t, TILES)
    scratch += both((), t, TILES) + [vm(NZ, 3, *t), vm(NZ, 3, *t)]
    scratch += both((NX,), t, TILES) + both((NX,), t, TILES)
    scratch += both((), (D,), ROWS, F32)
    scratch += both((ND,), (D,), SLOTS) + both((ND,), (D,), SLOTS)
    scratch += both((4,), (D,), SLOTS) + both((4,), (D,), SLOTS) + both((4,), (D,), SLOTS)
    scratch += both((NX,), t, TILES) + both((NX,), t, TILES)
    scratch += both((), (D,), ROWS, F32)
    scratch += [vm(NZ * w, 128, dtype=F32) for w in OUTS]
    scratch += both((NZ,), (128,), OUTS) + both((NZ,), (128,), OUTS)
    scratch += [vm(8, D, dtype=F32)]
    return pl.pallas_call(
        kernel,
        out_shape=(jax.ShapeDtypeStruct((2, D), BF16), jax.ShapeDtypeStruct((1, D), BF16)),
        in_specs=[HB] * 13 + [VM, VM, SM] + [VM] * 6,
        out_specs=(VM, VM),
        scratch_shapes=scratch,
        compiler_params=pltpu.CompilerParams(
            vmem_limit_bytes=VMEM_LIMIT, collective_id=0, has_side_effects=True
        ),
        name="two_steps",
    )(
        *heavy,
        attention_gain.reshape(1, D), decay_bias.reshape(1, H), decay_log,
        beta_weight.reshape(1, D), output_gain.reshape(1, H), expert_gain.reshape(1, D),
        tail_ids.reshape(1, 256), routes, tail_routes,
    )


def solution(mesh):
    placed = (
        P("dp", None),
        P("dp", None),
        P("dp", "expert", None, None),
        P(),
        P(),
        P(),
        P(),
        P(None, "expert"),
        P(None, "expert"),
        P(None, "expert"),
        P(),
        P(None, "expert"),
        P("expert"),
        P("expert"),
        P(None, "expert"),
        P(),
        P("expert", None),
        P(),
        P(),
        P("expert", None, "dp"),
        P("expert", None, "dp"),
        P("expert", "dp", None),
    )
    return jax.shard_map(
        on_device,
        mesh=mesh,
        in_specs=placed,
        out_specs=(P(("dp", "expert"), None), P(("dp", "expert"), None)),
        check_vma=False,
    )
```

```python
import functools

import jax
import jax.numpy as jnp
from jax import lax
from jax.experimental import pallas as pl
from jax.experimental.pallas import tpu as pltpu
from jax.sharding import PartitionSpec as P

F32 = jnp.float32
BF16 = jnp.bfloat16
EPS = 1e-06
ROUTE_SCALE = 2.446
MESH = pl.DeviceIdType.MESH
VMEM_LIMIT = 56 * 1024 * 1024
D = 2304
H = 128
NCT = D // 128
R1 = 64
R2 = 32
RT = R1 + R2
ND = 8
NX = 4
NZ = 8
ROWS = (64, 32)
SLOTS = (32, 16)
TILES = (18, 9)
OWNERS = (6, 3)
OUTS = (48, 32)
AX, AZ, BZ, BX, CC, DP, DY, EX, EZ = range(0, 18, 2)
KINDS = 18
PACK, HEAD = 2 * KINDS, 2 * KINDS + 2
SEM_ROWS = 2 * KINDS + 4


def iota(shape, dim):
    return lax.broadcasted_iota(jnp.int32, shape, dim)


def dot(a, b, contract=((1,), (0,)), precision=None):
    return lax.dot_general(
        a, b, (contract, ((), ())), precision=precision, preferred_element_type=F32
    )


def rms(wide, gain):
    factor = lax.rsqrt(jnp.mean(wide * wide, axis=-1, keepdims=True) + EPS)
    return wide * factor * gain


def cols(c):
    return slice(c * 128, c * 128 + 128)


def each(lo, hi, body):
    def step(k, carry):
        body(k)
        return carry

    lax.fori_loop(lo, hi, step, 0)


def kernel(
    x1h, x2h, sth, wqh, wkh, wvh, wddh, wduh, woh, roh, wgh, wuh, wdh,
    again, bias, dlog, wb, og, egain, ids, routes1, routes2,
    final,
    x1, x2, st, wall, wdu, wo, ro, wgu, wd,
    lsem, ssem, sem,
    normed, p1, p2all, named, tp, fresh, h1s, h2s, blk, h2c, h2r,
    ax_s1, ax_s2, ax_r1, ax_r2, az_s1, az_s2, az_r1, az_r2,
    rt1, rt2, hb1, hb2, hid1, hid2,
    slots1, slots2, out1, out2, pr1, pr2, zb1, zb2, zr1, zr2,
    ex_s1, ex_s2, ex_r1, ex_r2, res1, res2,
    scr1, scr2, ez_s1, ez_s2, ez_r1, ez_r2, rows,
):
    ax_s, ax_r, az_s, az_r = (ax_s1, ax_s2), (ax_r1, ax_r2), (az_s1, az_s2), (az_r1, az_r2)
    rt, hb, hid = (rt1, rt2), (hb1, hb2), (hid1, hid2)
    slots, out, pr, zb, zr = (slots1, slots2), (out1, out2), (pr1, pr2), (zb1, zb2), (zr1, zr2)
    ex_s, ex_r, res, scr = (ex_s1, ex_s2), (ex_r1, ex_r2), (res1, res2), (scr1, scr2)
    ez_s, ez_r = (ez_s1, ez_s2), (ez_r1, ez_r2)
    dp = lax.axis_index("dp")
    ex = lax.axis_index("expert")
    y = dp // 2
    core = lax.rem(dp, 2)
    xx = ex // NZ
    z = lax.rem(ex, NZ)

    def same(s):
        return 2 * lax.rem(y + s, 4) + core

    def other(s):
        return 2 * lax.rem(y + s, 4) + 1 - core

    def xat(s):
        return lax.rem(xx + s, NX)

    def zat(s):
        return lax.rem(z + s, NZ)

    def xdev(s):
        return {"expert": xat(s) * NZ + z}

    def zdev(s):
        return {"expert": xx * NZ + zat(s)}

    def rcopy(src, dst, row, snd, rcv, device):
        return pltpu.make_async_remote_copy(
            src_ref=src,
            dst_ref=dst,
            send_sem=sem.at[row, snd],
            recv_sem=sem.at[row + 1, rcv],
            device_id=device,
            device_id_type=MESH,
        )

    sent = []

    def send(make):
        make().start()
        sent.append(lambda: make().wait_send())

    def send_if(where, make):
        pl.when(where)(lambda: make().start())
        sent.append(lambda: pl.when(where)(lambda: make().wait_send()))

    loads = []
    for n, (src, dst) in enumerate(
        (
            (x2h, x2), (x1h, x1), (wqh, wall.at[:, pl.ds(0, H)]),
            (wkh, wall.at[:, pl.ds(H, H)]), (wvh, wall.at[:, pl.ds(2 * H, H)]),
            (wddh, wall.at[:, pl.ds(3 * H, H)]), (wduh, wdu),
        )
    ):
        loads.append(pltpu.make_async_copy(src, dst, lsem.at[n]))

    def load_state(i):
        part = pl.ds(i * 8, 8)
        return pltpu.make_async_copy(sth.at[part], st.at[part], ssem.at[i])

    later = []
    for n, (src, dst) in enumerate(((woh, wo), (roh, ro), (wgh, wgu.at[:, :, pl.ds(0, H)]), (wuh, wgu.at[:, :, pl.ds(H, H)]), (wdh, wd))):
        later.append(pltpu.make_async_copy(src, dst, lsem.at[7 + n]))
    for copy in loads:
        copy.start()
    barrier = pltpu.get_barrier_semaphore()
    for s in range(1, ND):
        pl.semaphore_signal(barrier, inc=1, device_id={"dp": lax.rem(dp + s, ND)}, device_id_type=MESH)
    for s in range(1, NX):
        pl.semaphore_signal(barrier, inc=1, device_id=xdev(s), device_id_type=MESH)
    for s in range(1, NZ):
        pl.semaphore_signal(barrier, inc=1, device_id=zdev(s), device_id_type=MESH)

    def load_block(k):
        block = xat(k + 1)
        load_state(2 * block).start()
        load_state(2 * block + 1).start()

    each(0, NX, load_block)
    later[0].start()
    load_wo, load_ro = later[0], later[1]

    again_row = again[...].reshape(1, D)
    egain_row = egain[...].reshape(1, D)
    for copy in loads:
        copy.wait()
    for copy in later[1:]:
        copy.start()
    normed[0:R1, :] = rms(x1[...].astype(F32), again_row).astype(BF16)
    normed[R1:RT, :] = rms(x2[...].astype(F32), again_row).astype(BF16)
    n = normed[...]
    every = dot(n, wall[...])

    def project(c):
        produced = every[:, cols(c)]
        return produced * jax.nn.sigmoid(produced)

    def unit(v):
        return v * lax.rsqrt(jnp.sum(v * v, axis=-1, keepdims=True) + EPS)

    q = unit(project(0))
    k = unit(project(1))
    v = project(2)
    low = every[:, cols(3)].astype(BF16)
    gate = dot(low, wdu[...]) + bias[...]
    soft = jnp.maximum(gate, 0.0) + jnp.log(1.0 + jnp.exp(-jnp.abs(gate)))
    strength = jnp.exp(jnp.full((RT, H), dlog[0], F32))
    decay = jnp.exp(-(strength * soft))
    beta = jax.nn.sigmoid(
        jnp.sum(n.astype(F32) * wb[...].astype(F32), axis=-1, keepdims=True)
    )
    dk = decay * k
    dq = decay * q
    sc = jnp.broadcast_to(beta * jnp.sum(k * q, axis=-1, keepdims=True), (RT, H))
    for c, part in enumerate((dk, dq, v, sc)):
        p2all[dp, :, cols(c)] = part[R1:RT, :].astype(BF16)
    pl.semaphore_wait(barrier, ND + NX + NZ - 3)

    def pack_copy(s, slot):
        return rcopy(
            p2all.at[dp], p2all.at[slot], PACK, s, slot, {"dp": lax.rem(dp + s, ND)}
        )

    each(1, ND, lambda s: pack_copy(s, dp).start())
    sent.append(lambda: each(1, ND, lambda s: pack_copy(s, dp).wait_send()))
    dk_hi = dk.astype(BF16).astype(F32)
    dq_hi = dq.astype(BF16).astype(F32)
    parts = (dk_hi, dk - dk_hi, dq_hi, dq - dq_hi, v, sc, decay, beta * k)
    for c, part in enumerate(parts):
        p1[:, cols(c)] = part[0:R1, :]

    m = iota((16, H), 0)

    def first_block(i):
        load_state(i).wait()
        at = pl.ds(pl.multiple_of(i * 8, 8), 8)
        t = p1[at, :]
        dcol = jnp.transpose(t[:, cols(6)])
        bcol = jnp.transpose(t[:, cols(7)])
        for j in range(8):
            row = [t[j : j + 1, cols(c)] for c in range(6)]
            state = st[i * 8 + j]
            a = jnp.where(m == 0, row[0], jnp.where(m == 1, row[1], jnp.where(m == 2, row[2], row[3])))
            got = dot(a.astype(BF16), state)
            u = row[4] - (got[0:1] + got[1:2])
            blk[j : j + 1, :] = got[2:3] + got[3:4] + row[5] * u
            fresh[i * 8 + j] = (
                state.astype(F32) * dcol[:, j : j + 1] + bcol[:, j : j + 1] * u
            ).astype(BF16)
        h1s[at, :] = rms(blk[...] * H**-0.5, og[...])

    order = iota((R1, R1), 0)
    within = order & 15
    source = order - within + jnp.where(within < 8, 2 * within, 2 * (within - 8) + 1)
    perm = (iota((R1, R1), 1) == source).astype(BF16)
    perm16 = perm[0:16, 0:16]

    def tile(p, val, xi, c):
        if p == 0:
            return val[xi * 16 : xi * 16 + 16, cols(c)]
        return jnp.concatenate(
            [val[xi * 8 : xi * 8 + 8, cols(2 * c)], val[xi * 8 : xi * 8 + 8, cols(2 * c + 1)]], axis=0
        )

    def a_send(p, val):
        for xi in range(NX):
            for c in range(TILES[p]):
                ax_s[p][xi, c] = tile(p, val, xi, c).astype(BF16)
        for s in (2, 1, 3):
            send(functools.partial(ax_copy, p, s, xx))

    def ax_copy(p, s, slot):
        return rcopy(ax_s[p].at[xat(s)], ax_r[p].at[slot], AX + KINDS * p, s, slot, xdev(s))

    def az_copy(p, s, slot):
        return rcopy(
            az_s[p].at[pl.ds(3 * zat(s), 3)], az_r[p].at[slot], AZ + KINDS * p, s, slot, zdev(s)
        )

    def az_own(p, slot):
        return rcopy(
            az_s[p].at[pl.ds(0, 3)], az_r[p].at[slot], AZ + KINDS * p, 0, slot, zdev(0)
        )

    def bz_copy(p, s, owner):
        part = hb[p].at[xx, pl.ds(3 * owner, 3)]
        return rcopy(part, part, BZ + KINDS * p, s, owner, zdev(s))

    def bx_copy(p, s, owner):
        part = hb[p].at[owner]
        return rcopy(part, part, BX + KINDS * p, s, owner, xdev(s))

    def a_turn(p):
        total = ax_s[p][xx].astype(F32)
        for s in (3, 2, 1):
            ax_copy(p, s, xat(s)).wait_recv()
            total = total + ax_r[p][xat(s)].astype(F32)
        az_s[p][...] = total.astype(BF16)
        for s in (4, 3, 5, 2, 6, 1, 7):
            send_if(zat(s) < OWNERS[p], functools.partial(az_copy, p, s, z))

    def b_start(p):
        @pl.when(z < OWNERS[p])
        def _():
            mine = pl.ds(3 * z, 3)
            total = az_s[p][mine].astype(F32) + rt[p][xx, mine].astype(F32)
            for s in (1, 7, 2, 6, 3, 5, 4):
                az_own(p, zat(s)).wait_recv()
                total = total + az_r[p][zat(s)].astype(F32)
            hb[p][xx, mine] = total.astype(BF16)
            for s in (4, 3, 5, 2, 6, 1, 7):
                bz_copy(p, s, z).start()

        def left():
            for s in range(1, NZ):
                bz_copy(p, s, z).wait_send()

        sent.append(lambda: pl.when(z < OWNERS[p])(left))

    def b_turn(p):
        for s in (1, 7, 2, 6, 3, 5, 4):

            @pl.when(zat(s) < OWNERS[p])
            def _():
                bz_copy(p, s, zat(s)).wait_recv()

        for s in (2, 1, 3):
            send(functools.partial(bx_copy, p, s, xx))

    def b_end(p):
        for s in (1, 3, 2):
            bx_copy(p, s, xat(s)).wait_recv()
        for xi in range(NX):
            for c in range(TILES[p]):
                got = hb[p][xi, c].astype(F32)
                if p == 0:
                    hid1[xi * 16 : xi * 16 + 16, cols(c)] = got
                else:
                    hid2[xi * 8 : xi * 8 + 8, cols(2 * c)] = got[0:8]
                    hid2[xi * 8 : xi * 8 + 8, cols(2 * c + 1)] = got[8:16]

    load_wo.wait()

    def first_x(k):
        s = lax.rem(k + 1, NX)
        xi = xat(s)
        each(0, 2, lambda b: first_block(2 * xi + b))
        h16 = h1s[pl.ds(pl.multiple_of(xi * 16, 16), 16), :].astype(BF16)
        val = dot(dot(perm16, h16).astype(BF16), wo[...])
        for c in range(NCT):
            ax_s1[xi, c] = val[:, cols(c)].astype(BF16)

        @pl.when(k < NX - 1)
        def _():
            ax_copy(0, s, xx).start()

    each(0, NX, first_x)
    sent.append(lambda: each(1, NX, lambda s: ax_copy(0, s, xx).wait_send()))

    base = dp * R1
    named[...] = (ids[...] == base + iota((R1, 256), 0)).astype(F32)
    for s in range(1, ND):
        pack_copy(s, lax.rem(dp + s, ND)).wait_recv()
    tp[...] = dot(named[...].astype(BF16), p2all[...].reshape(ND * R2, 4 * H))

    def second_block(i):
        at = pl.ds(pl.multiple_of(i * 8, 8), 8)
        t = tp[at, :]
        for j in range(8):
            row = [t[j : j + 1, cols(c)] for c in range(4)]
            a = jnp.where(m == 0, row[0], row[1])
            got = dot(a.astype(BF16), fresh[i * 8 + j])
            blk[j : j + 1, :] = got[1:2] + row[3] * (row[2] - got[0:1])
        h2s[at, :] = rms(blk[...] * H**-0.5, og[...])

    each(0, 8, second_block)
    h2c[...] = dot(named[...].astype(BF16), h2s[...].astype(BF16), ((0,), (0,))).astype(
        BF16
    ).reshape(ND, R2, H)

    def head_copy(s, slot):
        peer = lax.rem(dp + s, ND)
        return rcopy(h2c.at[peer], h2r.at[slot], HEAD, s, slot, {"dp": peer})

    each(1, ND, lambda s: head_copy(s, dp).start())
    sent.append(lambda: each(1, ND, lambda s: head_copy(s, dp).wait_send()))

    xp = dot(perm, x1[...])
    x2v = x2[...].astype(F32)
    for xi in range(NX):
        for c in range(TILES[0]):
            rt1[xi, c] = tile(0, xp, xi, c).astype(BF16)
        for c in range(TILES[1]):
            rt2[xi, c] = tile(1, x2v, xi, c).astype(BF16)
    a_turn(0)

    def multi_hot(tab, count):
        hot = jnp.zeros((count, 128), F32)
        for c in range(8):
            hot = hot + (tab[:, c : c + 1] == iota((count, 128), 1).astype(F32)).astype(F32)
        return hot

    def own_table(table, count):
        per = 128 // count
        lanes = pl.ds(pl.multiple_of(dp // per * 128, 128), 128)
        turned = jnp.transpose(table[:, lanes].astype(F32))
        got = turned[0:count]
        for g in range(1, per):
            got = jnp.where(lax.rem(dp, per) == g, turned[g * count : g * count + count], got)
        return got

    tab1, tab2 = own_table(routes1, R1), own_table(routes2, R2)
    mask = (dot(perm, multi_hot(tab1, R1).astype(BF16)), multi_hot(tab2, R2))
    expert_a, select, place = [], [], []
    for p in range(2):
        r, n_slots, cap = ROWS[p], SLOTS[p], (3, 2)[p]
        tri = (iota((r, r), 0) >= iota((r, r), 1)).astype(BF16)
        rank = (mask[p] * dot(tri, mask[p].astype(BF16))).astype(BF16)
        sa, sb = iota((128, n_slots), 1), iota((n_slots, 128), 0)
        hot_a = iota((128, n_slots), 0) == 4 * ex + (sa >> cap)
        hot_b = iota((n_slots, 128), 1) == 4 * ex + (sb >> cap)
        at_a = (iota((r, n_slots), 1) & ((1 << cap) - 1)) + 1
        at_b = (iota((n_slots, r), 0) & ((1 << cap) - 1)) + 1
        expert_a.append(hot_a.astype(F32))
        place.append((dot(rank, hot_a.astype(BF16)) == at_a.astype(F32)).astype(F32))
        select.append((dot(hot_b.astype(BF16), rank, ((1,), (1,))) == at_b.astype(F32)).astype(BF16))

    for s in range(1, ND):
        head_copy(s, lax.rem(dp + s, ND)).wait_recv()
    h2r[dp] = h2c[dp]
    heads2 = h2r[0].astype(F32)
    for g in range(1, ND):
        heads2 = heads2 + h2r[g].astype(F32)
    a_send(1, dot(heads2.astype(BF16), wo[...]))
    b_start(0)
    a_turn(1)
    b_turn(0)
    b_start(1)

    def c_copy(p, slot, row, device):
        part = slots[p].at[slot]
        return rcopy(part, part, CC + KINDS * p, row, slot, {"dp": device})

    def c_start(p):
        normed_p = rms(hid[p][...], egain_row).astype(BF16)
        slots[p][dp] = dot(select[p], normed_p).astype(BF16)
        for s in (2, 1, 3):
            send(functools.partial(c_copy, p, dp, s, same(s)))
        send(functools.partial(c_copy, p, dp, 0, other(0)))
        return normed_p

    def c_turn(p):
        for s in (1, 3, 2):
            c_copy(p, same(s), s, same(s)).wait_recv()
            send(functools.partial(c_copy, p, same(s), 3 + s, other(0)))

    def c_end(p):
        for s in (0, 1, 3, 2):
            c_copy(p, other(s), 0, other(0)).wait_recv()

    def weights(p, normed_p):
        scores = jax.nn.sigmoid(dot(normed_p, ro[...])) * mask[p]
        shares = ROUTE_SCALE * scores / jnp.sum(scores, axis=-1, keepdims=True)
        return dot(shares, expert_a[p], precision=lax.Precision.HIGHEST) * place[p]

    b_end(0)
    n0 = c_start(0)
    b_turn(1)
    load_ro.wait()
    w0 = weights(0, n0)
    b_end(1)
    n1 = c_start(1)
    w1 = weights(1, n1)
    share = (w0, w1)
    for copy in later[2:]:
        copy.wait()

    def hidden_units(x, e, mine):
        both = dot(x, wgu[e])
        g, u = both[:, 0:H], both[:, H : 2 * H]
        return jnp.where(mine, g * jax.nn.sigmoid(g) * u, 0.0).astype(BF16)

    spot = iota((ND * 16, H), 0) & 15

    def experts(p):
        if p == 0:
            for pair in range(2):
                x = slots1[:, 16 * pair : 16 * pair + 16, :].reshape(ND * 16, D)
                a0 = hidden_units(x, 2 * pair, (spot >> 3) == 0)
                a1 = hidden_units(x, 2 * pair + 1, (spot >> 3) == 1)
                for c in range(0, D, 768):
                    cc = slice(c, c + 768)
                    got = dot(a0, wd[2 * pair, :, cc]) + dot(a1, wd[2 * pair + 1, :, cc])
                    out1[:, 16 * pair : 16 * pair + 16, cc] = got.astype(BF16).reshape(ND, 16, 768)
        else:
            x = slots2[...].reshape(ND * 16, D)
            acts = [hidden_units(x, e, (spot >> 2) == e) for e in range(4)]
            for c in range(0, D, 768):
                cc = slice(c, c + 768)
                got = dot(acts[0], wd[0, :, cc])
                for e in range(1, 4):
                    got = got + dot(acts[e], wd[e, :, cc])
                out2[:, :, cc] = got.astype(BF16).reshape(ND, 16, 768)

    def pair_copy(p, s):
        yy = lax.rem(y + s, 4)
        return rcopy(out[p].at[other(s)], pr[p].at[yy], DP + KINDS * p, yy, yy, {"dp": other(0)})

    def chip_copy(p, s, slot):
        yy = lax.rem(y + s, 4)
        return rcopy(zb[p].at[yy], zr[p].at[slot], DY + KINDS * p, yy, slot, {"dp": same(s)})

    def d_start(p):
        for s in (2, 1, 3, 0):
            send(functools.partial(pair_copy, p, s))

    def d_turn(p):
        for s in (2, 1, 3):
            yy = lax.rem(y + s, 4)
            pair_copy(p, s).wait_recv()
            zb[p][yy] = (out[p][same(s)].astype(F32) + pr[p][yy].astype(F32)).astype(BF16)
            send(functools.partial(chip_copy, p, s, y))
        pair_copy(p, 0).wait_recv()

    def ex_copy(p, s, slot):
        return rcopy(ex_s[p].at[xat(s)], ex_r[p].at[slot], EX + KINDS * p, s, slot, xdev(s))

    def ez_copy(p, s, slot):
        return rcopy(ez_s[p].at[zat(s)], ez_r[p].at[slot], EZ + KINDS * p, s, slot, zdev(s))

    def e_start(p):
        total = out[p][dp].astype(F32) + pr[p][y].astype(F32)
        for s in (1, 3, 2):
            yy = lax.rem(y + s, 4)
            chip_copy(p, s, yy).wait_recv()
            total = total + zr[p][yy].astype(F32)
        summed = total.astype(BF16)
        w_hi = share[p].astype(BF16)
        w_lo = (share[p] - w_hi.astype(F32)).astype(BF16)
        got = dot(w_hi, summed) + dot(w_lo, summed)
        res[p][...] = got
        for xi in range(NX):
            for c in range(TILES[p]):
                ex_s[p][xi, c] = tile(p, got, xi, c).astype(BF16)
        for s in (2, 1, 3):
            send(functools.partial(ex_copy, p, s, xx))

    def e_turn(p):
        block = (16, 8)[p]
        at = pl.ds(pl.multiple_of(xx * block, block), block)
        own = (iota((block, 128), 0) & 7) == z
        for s in (1, 3, 2):
            ex_copy(p, s, xat(s)).wait_recv()
        scr[p][...] = jnp.zeros_like(scr[p])
        for c in range(TILES[p]):
            arrived = ex_r[p][xat(1), c].astype(F32)
            for s in (2, 3):
                arrived = arrived + ex_r[p][xat(s), c].astype(F32)
            for half in range(2):
                ct = c if p == 0 else 2 * c + half
                if p == 0 and half == 1:
                    continue
                mine = res[p][at, cols(ct)] + jnp.where(own, hid[p][at, cols(ct)], 0.0)
                if p == 0:
                    val = mine + arrived
                    scr1[pl.ds(ct, NZ, stride=48), :] = val[0:8]
                    scr1[pl.ds(NCT + ct, NZ, stride=48), :] = val[8:16]
                else:
                    scr2[pl.ds(ct, NZ, stride=32), :] = mine + arrived[8 * half : 8 * half + 8]
        w = OUTS[p]
        for zi in range(NZ):
            ez_s[p][zi] = scr[p][zi * w : zi * w + w, :].astype(BF16)
        for s in (4, 3, 5, 2, 6, 1, 7):
            send(functools.partial(ez_copy, p, s, z))

    def e_end(p):
        w = OUTS[p]
        total = scr[p][pl.ds(pl.multiple_of(z * w, w), w), :]
        for s in (1, 7, 2, 6, 3, 5, 4):
            ez_copy(p, s, zat(s)).wait_recv()
            total = total + ez_r[p][zat(s)].astype(F32)
        for j in range(2 - p):
            for ct in range(NCT):
                rows[2 * p + j : 2 * p + j + 1, cols(ct)] = total[j * NCT + ct : j * NCT + ct + 1, :]

    c_turn(0)
    c_end(0)
    experts(0)
    d_start(0)
    c_turn(1)
    d_turn(0)
    c_end(1)
    experts(1)
    d_start(1)
    d_turn(1)
    e_start(0)
    e_start(1)
    e_turn(0)
    e_turn(1)
    e_end(0)
    e_end(1)
    final[...] = rows[...]

    for left in sent:
        left()


def write_kernel(final, first, tail):
    first[...] = final[0:2, :].astype(BF16)
    tail[...] = final[2:3, :].astype(BF16)


VM = pl.BlockSpec(memory_space=pltpu.VMEM)
SM = pl.BlockSpec(memory_space=pltpu.SMEM)
HB = pl.BlockSpec(memory_space=pl.ANY)
DMA = pltpu.SemaphoreType.DMA


def on_device(
    inputs, tail_inputs, states, tail_ids, routes, tail_routes, attention_gain,
    query_weight, key_weight, value_weight, decay_down, decay_up, decay_bias,
    decay_log, beta_weight, output_gain, head_out, expert_gain, router_weight,
    gate_weight, up_weight, down_weight,
):
    def vm(*dims, dtype=BF16):
        return pltpu.VMEM(dims, dtype)

    def both(lead, rest, sizes, dtype=BF16):
        return [vm(*lead, n, *rest, dtype=dtype) for n in sizes]

    heavy = (
        inputs, tail_inputs, states.reshape(R1, H, H), query_weight, key_weight,
        value_weight, decay_down, decay_up, head_out, router_weight, gate_weight,
        up_weight, down_weight,
    )
    scratch = [
        vm(R1, D), vm(R2, D), vm(R1, H, H), vm(D, 4 * H), vm(H, H), vm(H, D), vm(D, 128),
        vm(4, D, 2 * H), vm(4, H, D),
    ]
    scratch += [DMA((12,)), DMA((8,)), DMA((SEM_ROWS, 8))]
    scratch += [
        vm(RT, D), vm(R1, 8 * H, dtype=F32), vm(ND, R2, 4 * H), vm(R1, 256, dtype=F32),
        vm(R1, 4 * H, dtype=F32), vm(R1, H, H), vm(R1, H, dtype=F32), vm(R1, H, dtype=F32),
        vm(8, H, dtype=F32), vm(ND, R2, H), vm(ND, R2, H),
    ]
    t = (16, 128)
    scratch += both((NX,), t, TILES) + both((NX,), t, TILES)
    scratch += both((), t, TILES) + [vm(NZ, 3, *t), vm(NZ, 3, *t)]
    scratch += both((NX,), t, TILES) + both((NX,), t, TILES)
    scratch += both((), (D,), ROWS, F32)
    scratch += both((ND,), (D,), SLOTS) + both((ND,), (D,), SLOTS)
    scratch += both((4,), (D,), SLOTS) + both((4,), (D,), SLOTS) + both((4,), (D,), SLOTS)
    scratch += both((NX,), t, TILES) + both((NX,), t, TILES)
    scratch += both((), (D,), ROWS, F32)
    scratch += [vm(NZ * w, 128, dtype=F32) for w in OUTS]
    scratch += both((NZ,), (128,), OUTS) + both((NZ,), (128,), OUTS)
    scratch += [vm(8, D, dtype=F32)]
    final = pl.pallas_call(
        kernel,
        out_shape=jax.ShapeDtypeStruct((8, D), F32),
        in_specs=[HB] * 13 + [VM, VM, SM] + [VM] * 6,
        out_specs=VM,
        scratch_shapes=scratch,
        compiler_params=pltpu.CompilerParams(
            vmem_limit_bytes=VMEM_LIMIT, collective_id=0, has_side_effects=True
        ),
        name="two_steps",
    )(
        *heavy,
        attention_gain, decay_bias.reshape(1, H), decay_log,
        beta_weight.reshape(1, D), output_gain.reshape(1, H), expert_gain,
        tail_ids.reshape(1, 256), routes.T, tail_routes.T,
    )
    return pl.pallas_call(
        write_kernel,
        out_shape=(jax.ShapeDtypeStruct((2, D), BF16), jax.ShapeDtypeStruct((1, D), BF16)),
        in_specs=[VM],
        out_specs=(VM, VM),
        name="write",
    )(final)


def solution(mesh):
    placed = (
        P("dp", None),
        P("dp", None),
        P("dp", "expert", None, None),
        P(),
        P(),
        P(),
        P(),
        P(None, "expert"),
        P(None, "expert"),
        P(None, "expert"),
        P(),
        P(None, "expert"),
        P("expert"),
        P("expert"),
        P(None, "expert"),
        P(),
        P("expert", None),
        P(),
        P(),
        P("expert", None, "dp"),
        P("expert", None, "dp"),
        P("expert", "dp", None),
    )
    return jax.shard_map(
        on_device,
        mesh=mesh,
        in_specs=placed,
        out_specs=(P(("dp", "expert"), None), P(("dp", "expert"), None)),
        check_vma=False,
    )
```

```python
import functools

import jax
import jax.numpy as jnp
from jax import lax
from jax.experimental import pallas as pl
from jax.experimental.pallas import tpu as pltpu
from jax.sharding import PartitionSpec as P

F32 = jnp.float32
BF16 = jnp.bfloat16
EPS = 1e-06
ROUTE_SCALE = 2.446
MESH = pl.DeviceIdType.MESH
VMEM_LIMIT = 56 * 1024 * 1024
D = 2304
H = 128
NCT = D // 128
R1 = 64
R2 = 32
SECOND = 16
RT = R1 + R2
ND = 8
NX = 4
NZ = 8
ROWS = (64, 32)
SLOTS = (32, 16)
TILES = (18, 9)
OWNERS = (6, 3)
OUTS = (48, 32)
AX, AZ, BZ, BX, CC, DP, DY, EX, EZ = range(0, 18, 2)
KINDS = 18
PACK, HEAD = 2 * KINDS, 2 * KINDS + 2
SEM_ROWS = 2 * KINDS + 4


def iota(shape, dim):
    return lax.broadcasted_iota(jnp.int32, shape, dim)


def dot(a, b, contract=((1,), (0,)), precision=None):
    return lax.dot_general(
        a, b, (contract, ((), ())), precision=precision, preferred_element_type=F32
    )


def rms(wide, gain):
    factor = lax.rsqrt(jnp.mean(wide * wide, axis=-1, keepdims=True) + EPS)
    return wide * factor * gain


def cols(c):
    return slice(c * 128, c * 128 + 128)


def each(lo, hi, body):
    def step(k, carry):
        body(k)
        return carry

    lax.fori_loop(lo, hi, step, 0)


def kernel(
    x1h, x2h, sth, wqh, wkh, wvh, wddh, wduh, woh, roh, wgh, wuh, wdh,
    again, bias, dlog, wb, og, egain, ids, routes1, routes2,
    final,
    x1, x2, st, wall, wdu, wo, ro, wgu, wd,
    lsem, ssem, sem,
    normed, p1, p2all, w2, named, tp, fresh, h2s, h2c, h2r,
    ax_s1, ax_s2, ax_r1, ax_r2, az_s1, az_s2, az_r1, az_r2,
    rt1, rt2, hb1, hb2, hid1, hid2,
    slots1, slots2, out1, out2, pr1, pr2, zb1, zb2, zr1, zr2,
    ex_s1, ex_s2, ex_r1, ex_r2, res1, res2,
    scr1, scr2, ez_s1, ez_s2, ez_r1, ez_r2, rows,
):
    ax_s, ax_r, az_s, az_r = (ax_s1, ax_s2), (ax_r1, ax_r2), (az_s1, az_s2), (az_r1, az_r2)
    rt, hb, hid = (rt1, rt2), (hb1, hb2), (hid1, hid2)
    slots, out, pr, zb, zr = (slots1, slots2), (out1, out2), (pr1, pr2), (zb1, zb2), (zr1, zr2)
    ex_s, ex_r, res, scr = (ex_s1, ex_s2), (ex_r1, ex_r2), (res1, res2), (scr1, scr2)
    ez_s, ez_r = (ez_s1, ez_s2), (ez_r1, ez_r2)
    dp = lax.axis_index("dp")
    ex = lax.axis_index("expert")
    y = dp // 2
    core = lax.rem(dp, 2)
    xx = ex // NZ
    z = lax.rem(ex, NZ)

    def same(s):
        return 2 * lax.rem(y + s, 4) + core

    def other(s):
        return 2 * lax.rem(y + s, 4) + 1 - core

    def xat(s):
        return lax.rem(xx + s, NX)

    def zat(s):
        return lax.rem(z + s, NZ)

    def xdev(s):
        return {"expert": xat(s) * NZ + z}

    def zdev(s):
        return {"expert": xx * NZ + zat(s)}

    def rcopy(src, dst, row, snd, rcv, device):
        return pltpu.make_async_remote_copy(
            src_ref=src,
            dst_ref=dst,
            send_sem=sem.at[row, snd],
            recv_sem=sem.at[row + 1, rcv],
            device_id=device,
            device_id_type=MESH,
        )

    sent = []

    def send(make):
        make().start()
        sent.append(lambda: make().wait_send())

    def send_if(where, make):
        pl.when(where)(lambda: make().start())
        sent.append(lambda: pl.when(where)(lambda: make().wait_send()))

    loads = []
    for n, (src, dst) in enumerate(
        (
            (x2h, x2), (x1h, x1), (wqh, wall.at[:, pl.ds(0, H)]),
            (wkh, wall.at[:, pl.ds(H, H)]), (wvh, wall.at[:, pl.ds(2 * H, H)]),
            (wddh, wall.at[:, pl.ds(3 * H, H)]), (wduh, wdu),
        )
    ):
        loads.append(pltpu.make_async_copy(src, dst, lsem.at[n]))

    def load_state(i):
        part = pl.ds(i * 8, 8)
        return pltpu.make_async_copy(sth.at[part], st.at[part], ssem.at[i])

    later = []
    for n, (src, dst) in enumerate(((woh, wo), (roh, ro), (wgh, wgu.at[:, :, pl.ds(0, H)]), (wuh, wgu.at[:, :, pl.ds(H, H)]), (wdh, wd))):
        later.append(pltpu.make_async_copy(src, dst, lsem.at[7 + n]))
    for copy in loads:
        copy.start()
    barrier = pltpu.get_barrier_semaphore()
    for s in range(1, ND):
        pl.semaphore_signal(barrier, inc=1, device_id={"dp": lax.rem(dp + s, ND)}, device_id_type=MESH)
    for s in range(1, NX):
        pl.semaphore_signal(barrier, inc=1, device_id=xdev(s), device_id_type=MESH)
    for s in range(1, NZ):
        pl.semaphore_signal(barrier, inc=1, device_id=zdev(s), device_id_type=MESH)

    def load_block(k):
        block = xat(k + 1)
        load_state(2 * block).start()
        load_state(2 * block + 1).start()

    each(0, NX, load_block)
    later[0].start()
    load_wo, load_ro = later[0], later[1]

    again_row = again[...].reshape(1, D)
    egain_row = egain[...].reshape(1, D)
    for copy in loads:
        copy.wait()
    for copy in later[1:]:
        copy.start()
    normed[0:R1, :] = rms(x1[...].astype(F32), again_row).astype(BF16)
    normed[R1:RT, :] = rms(x2[...].astype(F32), again_row).astype(BF16)
    n = normed[...]
    every = dot(n, wall[...])

    def project(c):
        produced = every[:, cols(c)]
        return produced * jax.nn.sigmoid(produced)

    def unit(v):
        return v * lax.rsqrt(jnp.sum(v * v, axis=-1, keepdims=True) + EPS)

    q = unit(project(0))
    k = unit(project(1))
    v = project(2)
    low = every[:, cols(3)].astype(BF16)
    gate = dot(low, wdu[...]) + bias[...]
    soft = jnp.maximum(gate, 0.0) + jnp.log(1.0 + jnp.exp(-jnp.abs(gate)))
    strength = jnp.exp(jnp.full((RT, H), dlog[0], F32))
    decay = jnp.exp(-(strength * soft))
    beta = jax.nn.sigmoid(
        jnp.sum(n.astype(F32) * wb[...].astype(F32), axis=-1, keepdims=True)
    )
    dk = decay * k
    dq = decay * q
    sc = jnp.broadcast_to(beta * jnp.sum(k * q, axis=-1, keepdims=True), (RT, H))
    p2all[dp] = (dq - sc * dk)[R1:RT, :].astype(BF16)
    w2[...] = (sc * v)[R1:RT, :]
    pl.semaphore_wait(barrier, ND + NX + NZ - 3)

    def pack_copy(s, slot):
        return rcopy(
            p2all.at[dp], p2all.at[slot], PACK, s, slot, {"dp": lax.rem(dp + s, ND)}
        )

    each(1, ND, lambda s: pack_copy(s, dp).start())
    sent.append(lambda: each(1, ND, lambda s: pack_copy(s, dp).wait_send()))
    dk_hi = dk.astype(BF16).astype(F32)
    dq_hi = dq.astype(BF16).astype(F32)
    parts = (dk_hi, dk - dk_hi, dq_hi, dq - dq_hi, v, sc, decay, beta * k)
    for c, part in enumerate(parts):
        p1[:, cols(c)] = part[0:R1, :]

    m = iota((16, H), 0)

    def first_rows(start, count):
        t = p1[pl.ds(pl.multiple_of(start, count), count), :]
        dcol = jnp.transpose(t[:, cols(6)])
        bcol = jnp.transpose(t[:, cols(7)])
        reads = []
        for j in range(count):
            row = [t[j : j + 1, cols(c)] for c in range(6)]
            state = st[start + j]
            a = jnp.where(m == 0, row[0], jnp.where(m == 1, row[1], jnp.where(m == 2, row[2], row[3])))
            got = dot(a.astype(BF16), state)
            u = row[4] - (got[0:1] + got[1:2])
            reads.append(got[2:3] + got[3:4] + row[5] * u)
            fresh[start + j] = (
                state.astype(F32) * dcol[:, j : j + 1] + bcol[:, j : j + 1] * u
            ).astype(BF16)
        return rms(jnp.concatenate(reads, axis=0) * H**-0.5, og[...])

    order = iota((R1, R1), 0)
    within = order & 15
    source = order - within + jnp.where(within < 8, 2 * within, 2 * (within - 8) + 1)
    perm = (iota((R1, R1), 1) == source).astype(BF16)
    perm16 = perm[0:16, 0:16]

    def tile(p, val, xi, c):
        if p == 0:
            return val[xi * 16 : xi * 16 + 16, cols(c)]
        return jnp.concatenate(
            [val[xi * 8 : xi * 8 + 8, cols(2 * c)], val[xi * 8 : xi * 8 + 8, cols(2 * c + 1)]], axis=0
        )

    def a_send(p, val):
        for xi in range(NX):
            for c in range(TILES[p]):
                ax_s[p][xi, c] = tile(p, val, xi, c).astype(BF16)
        for s in (2, 1, 3):
            send(functools.partial(ax_copy, p, s, xx))

    def ax_copy(p, s, slot):
        return rcopy(ax_s[p].at[xat(s)], ax_r[p].at[slot], AX + KINDS * p, s, slot, xdev(s))

    def az_copy(p, s, slot):
        return rcopy(
            az_s[p].at[pl.ds(3 * zat(s), 3)], az_r[p].at[slot], AZ + KINDS * p, s, slot, zdev(s)
        )

    def az_own(p, slot):
        return rcopy(
            az_s[p].at[pl.ds(0, 3)], az_r[p].at[slot], AZ + KINDS * p, 0, slot, zdev(0)
        )

    def bz_copy(p, s, owner):
        part = hb[p].at[xx, pl.ds(3 * owner, 3)]
        return rcopy(part, part, BZ + KINDS * p, s, owner, zdev(s))

    def bx_copy(p, s, owner):
        part = hb[p].at[owner]
        return rcopy(part, part, BX + KINDS * p, s, owner, xdev(s))

    def a_turn(p):
        total = ax_s[p][xx].astype(F32)
        for s in (3, 2, 1):
            ax_copy(p, s, xat(s)).wait_recv()
            total = total + ax_r[p][xat(s)].astype(F32)
        az_s[p][...] = total.astype(BF16)
        for s in (4, 3, 5, 2, 6, 1, 7):
            send_if(zat(s) < OWNERS[p], functools.partial(az_copy, p, s, z))

    def b_start(p):
        @pl.when(z < OWNERS[p])
        def _():
            mine = pl.ds(3 * z, 3)
            total = az_s[p][mine].astype(F32) + rt[p][xx, mine].astype(F32)
            for s in (1, 7, 2, 6, 3, 5, 4):
                az_own(p, zat(s)).wait_recv()
                total = total + az_r[p][zat(s)].astype(F32)
            hb[p][xx, mine] = total.astype(BF16)
            for s in (4, 3, 5, 2, 6, 1, 7):
                bz_copy(p, s, z).start()

        def left():
            for s in range(1, NZ):
                bz_copy(p, s, z).wait_send()

        sent.append(lambda: pl.when(z < OWNERS[p])(left))

    def b_turn(p):
        for s in (1, 7, 2, 6, 3, 5, 4):

            @pl.when(zat(s) < OWNERS[p])
            def _():
                bz_copy(p, s, zat(s)).wait_recv()

        for s in (2, 1, 3):
            send(functools.partial(bx_copy, p, s, xx))

    def b_end(p):
        for s in (1, 3, 2):
            bx_copy(p, s, xat(s)).wait_recv()
        for xi in range(NX):
            for c in range(TILES[p]):
                got = hb[p][xi, c].astype(F32)
                if p == 0:
                    hid1[xi * 16 : xi * 16 + 16, cols(c)] = got
                else:
                    hid2[xi * 8 : xi * 8 + 8, cols(2 * c)] = got[0:8]
                    hid2[xi * 8 : xi * 8 + 8, cols(2 * c + 1)] = got[8:16]

    load_wo.wait()

    def first_x(k):
        s = lax.rem(k + 1, NX)
        xi = xat(s)
        load_state(2 * xi).wait()
        load_state(2 * xi + 1).wait()
        h16 = first_rows(xi * 16, 16).astype(BF16)
        val = dot(dot(perm16, h16).astype(BF16), wo[...])
        for c in range(NCT):
            ax_s1[xi, c] = val[:, cols(c)].astype(BF16)

        @pl.when(k < NX - 1)
        def _():
            ax_copy(0, s, xx).start()

    each(0, NX, first_x)
    sent.append(lambda: each(1, NX, lambda s: ax_copy(0, s, xx).wait_send()))

    xp = dot(perm, x1[...])
    x2v = x2[...].astype(F32)
    for xi in range(NX):
        for c in range(TILES[0]):
            rt1[xi, c] = tile(0, xp, xi, c).astype(BF16)
        for c in range(TILES[1]):
            rt2[xi, c] = tile(1, x2v, xi, c).astype(BF16)
    def multi_hot(tab, count):
        hot = jnp.zeros((count, 128), F32)
        for c in range(8):
            hot = hot + (tab[:, c : c + 1] == iota((count, 128), 1).astype(F32)).astype(F32)
        return hot

    def own_table(table, count):
        per = 128 // count
        lanes = pl.ds(pl.multiple_of(dp // per * 128, 128), 128)
        turned = jnp.transpose(table[:, lanes].astype(F32))
        got = turned[0:count]
        for g in range(1, per):
            got = jnp.where(lax.rem(dp, per) == g, turned[g * count : g * count + count], got)
        return got

    tab1, tab2 = own_table(routes1, R1), own_table(routes2, R2)
    mask = (dot(perm, multi_hot(tab1, R1).astype(BF16)), multi_hot(tab2, R2))
    expert_a, select, place = [], [], []
    for p in range(2):
        r, n_slots, cap = ROWS[p], SLOTS[p], (3, 2)[p]
        tri = (iota((r, r), 0) >= iota((r, r), 1)).astype(BF16)
        rank = (mask[p] * dot(tri, mask[p].astype(BF16))).astype(BF16)
        sa, sb = iota((128, n_slots), 1), iota((n_slots, 128), 0)
        hot_a = iota((128, n_slots), 0) == 4 * ex + (sa >> cap)
        hot_b = iota((n_slots, 128), 1) == 4 * ex + (sb >> cap)
        at_a = (iota((r, n_slots), 1) & ((1 << cap) - 1)) + 1
        at_b = (iota((n_slots, r), 0) & ((1 << cap) - 1)) + 1
        expert_a.append(hot_a.astype(F32))
        place.append((dot(rank, hot_a.astype(BF16)) == at_a.astype(F32)).astype(F32))
        select.append((dot(hot_b.astype(BF16), rank, ((1,), (1,))) == at_b.astype(F32)).astype(BF16))

    base = dp * R1
    named[...] = (ids[...] == base + iota((R1, 256), 0)).astype(F32)
    for s in range(1, ND):
        pack_copy(s, lax.rem(dp + s, ND)).wait_recv()
    tp[...] = dot(named[...].astype(BF16), p2all[...].reshape(ND * R2, H))

    def second_rows(k):
        count = SECOND
        at = pl.ds(pl.multiple_of(k * count, count), count)
        t = tp[at, :]
        reads = []
        for j in range(count):
            a = jnp.broadcast_to(t[j : j + 1], (16, H))
            reads.append(dot(a.astype(BF16), fresh[k * count + j])[0:1])
        h2s[at, :] = jnp.concatenate(reads, axis=0)

    each(0, R1 // SECOND, second_rows)
    h2c[...] = dot(named[...].astype(BF16), h2s[...].astype(BF16), ((0,), (0,))).astype(
        BF16
    ).reshape(ND, R2, H)

    def head_copy(s, slot):
        peer = lax.rem(dp + s, ND)
        return rcopy(h2c.at[peer], h2r.at[slot], HEAD, s, slot, {"dp": peer})

    each(1, ND, lambda s: head_copy(s, dp).start())
    sent.append(lambda: each(1, ND, lambda s: head_copy(s, dp).wait_send()))

    a_turn(0)
    for s in range(1, ND):
        head_copy(s, lax.rem(dp + s, ND)).wait_recv()
    h2r[dp] = h2c[dp]
    heads2 = h2r[0].astype(F32)
    for g in range(1, ND):
        heads2 = heads2 + h2r[g].astype(F32)
    heads2 = rms((heads2 + w2[...]) * H**-0.5, og[...])
    a_send(1, dot(heads2.astype(BF16), wo[...]))
    b_start(0)
    a_turn(1)
    b_turn(0)
    b_start(1)

    def c_copy(p, slot, row, device):
        part = slots[p].at[slot]
        return rcopy(part, part, CC + KINDS * p, row, slot, {"dp": device})

    def c_start(p):
        normed_p = rms(hid[p][...], egain_row).astype(BF16)
        slots[p][dp] = dot(select[p], normed_p).astype(BF16)
        for s in (2, 1, 3):
            send(functools.partial(c_copy, p, dp, s, same(s)))
        send(functools.partial(c_copy, p, dp, 0, other(0)))
        return normed_p

    def c_turn(p):
        for s in (1, 3, 2):
            c_copy(p, same(s), s, same(s)).wait_recv()
            send(functools.partial(c_copy, p, same(s), 3 + s, other(0)))

    def c_end(p):
        for s in (0, 1, 3, 2):
            c_copy(p, other(s), 0, other(0)).wait_recv()

    def weights(p, normed_p):
        scores = jax.nn.sigmoid(dot(normed_p, ro[...])) * mask[p]
        shares = ROUTE_SCALE * scores / jnp.sum(scores, axis=-1, keepdims=True)
        return dot(shares, expert_a[p], precision=lax.Precision.HIGHEST) * place[p]

    b_end(0)
    n0 = c_start(0)
    b_turn(1)
    load_ro.wait()
    w0 = weights(0, n0)
    b_end(1)
    n1 = c_start(1)
    w1 = weights(1, n1)
    share = (w0, w1)
    for copy in later[2:]:
        copy.wait()

    def hidden_units(x, e, mine):
        both = dot(x, wgu[e])
        g, u = both[:, 0:H], both[:, H : 2 * H]
        return jnp.where(mine, g * jax.nn.sigmoid(g) * u, 0.0).astype(BF16)

    spot = iota((ND * 16, H), 0) & 15

    def experts(p):
        if p == 0:
            for pair in range(2):
                x = slots1[:, 16 * pair : 16 * pair + 16, :].reshape(ND * 16, D)
                a0 = hidden_units(x, 2 * pair, (spot >> 3) == 0)
                a1 = hidden_units(x, 2 * pair + 1, (spot >> 3) == 1)
                for c in range(0, D, 768):
                    cc = slice(c, c + 768)
                    got = dot(a0, wd[2 * pair, :, cc]) + dot(a1, wd[2 * pair + 1, :, cc])
                    out1[:, 16 * pair : 16 * pair + 16, cc] = got.astype(BF16).reshape(ND, 16, 768)
        else:
            x = slots2[...].reshape(ND * 16, D)
            acts = [hidden_units(x, e, (spot >> 2) == e) for e in range(4)]
            for c in range(0, D, 768):
                cc = slice(c, c + 768)
                got = dot(acts[0], wd[0, :, cc])
                for e in range(1, 4):
                    got = got + dot(acts[e], wd[e, :, cc])
                out2[:, :, cc] = got.astype(BF16).reshape(ND, 16, 768)

    def pair_copy(p, s):
        yy = lax.rem(y + s, 4)
        return rcopy(out[p].at[other(s)], pr[p].at[yy], DP + KINDS * p, yy, yy, {"dp": other(0)})

    def chip_copy(p, s, slot):
        yy = lax.rem(y + s, 4)
        return rcopy(zb[p].at[yy], zr[p].at[slot], DY + KINDS * p, yy, slot, {"dp": same(s)})

    def d_start(p):
        for s in (2, 1, 3, 0):
            send(functools.partial(pair_copy, p, s))

    def d_turn(p):
        for s in (2, 1, 3):
            yy = lax.rem(y + s, 4)
            pair_copy(p, s).wait_recv()
            zb[p][yy] = (out[p][same(s)].astype(F32) + pr[p][yy].astype(F32)).astype(BF16)
            send(functools.partial(chip_copy, p, s, y))
        pair_copy(p, 0).wait_recv()

    def ex_copy(p, s, slot):
        return rcopy(ex_s[p].at[xat(s)], ex_r[p].at[slot], EX + KINDS * p, s, slot, xdev(s))

    def ez_copy(p, s, slot):
        return rcopy(ez_s[p].at[zat(s)], ez_r[p].at[slot], EZ + KINDS * p, s, slot, zdev(s))

    def e_start(p):
        total = out[p][dp].astype(F32) + pr[p][y].astype(F32)
        for s in (1, 3, 2):
            yy = lax.rem(y + s, 4)
            chip_copy(p, s, yy).wait_recv()
            total = total + zr[p][yy].astype(F32)
        summed = total.astype(BF16)
        w_hi = share[p].astype(BF16)
        w_lo = (share[p] - w_hi.astype(F32)).astype(BF16)
        got = dot(w_hi, summed) + dot(w_lo, summed)
        res[p][...] = got
        for xi in range(NX):
            for c in range(TILES[p]):
                ex_s[p][xi, c] = tile(p, got, xi, c).astype(BF16)
        for s in (2, 1, 3):
            send(functools.partial(ex_copy, p, s, xx))

    def e_turn(p):
        block = (16, 8)[p]
        at = pl.ds(pl.multiple_of(xx * block, block), block)
        own = (iota((block, 128), 0) & 7) == z
        for s in (1, 3, 2):
            ex_copy(p, s, xat(s)).wait_recv()
        scr[p][...] = jnp.zeros_like(scr[p])
        for c in range(TILES[p]):
            arrived = ex_r[p][xat(1), c].astype(F32)
            for s in (2, 3):
                arrived = arrived + ex_r[p][xat(s), c].astype(F32)
            for half in range(2):
                ct = c if p == 0 else 2 * c + half
                if p == 0 and half == 1:
                    continue
                mine = res[p][at, cols(ct)] + jnp.where(own, hid[p][at, cols(ct)], 0.0)
                if p == 0:
                    val = mine + arrived
                    scr1[pl.ds(ct, NZ, stride=48), :] = val[0:8]
                    scr1[pl.ds(NCT + ct, NZ, stride=48), :] = val[8:16]
                else:
                    scr2[pl.ds(ct, NZ, stride=32), :] = mine + arrived[8 * half : 8 * half + 8]
        w = OUTS[p]
        for zi in range(NZ):
            ez_s[p][zi] = scr[p][zi * w : zi * w + w, :].astype(BF16)
        for s in (4, 3, 5, 2, 6, 1, 7):
            send(functools.partial(ez_copy, p, s, z))

    def e_end(p):
        w = OUTS[p]
        total = scr[p][pl.ds(pl.multiple_of(z * w, w), w), :]
        for s in (1, 7, 2, 6, 3, 5, 4):
            ez_copy(p, s, zat(s)).wait_recv()
            total = total + ez_r[p][zat(s)].astype(F32)
        for j in range(2 - p):
            for ct in range(NCT):
                rows[2 * p + j : 2 * p + j + 1, cols(ct)] = total[j * NCT + ct : j * NCT + ct + 1, :]

    c_turn(0)
    c_end(0)
    experts(0)
    d_start(0)
    c_turn(1)
    d_turn(0)
    c_end(1)
    experts(1)
    d_start(1)
    d_turn(1)
    e_start(0)
    e_start(1)
    e_turn(0)
    e_turn(1)
    e_end(0)
    e_end(1)
    final[...] = rows[...]

    for left in sent:
        left()


def write_kernel(final, first, tail):
    first[...] = final[0:2, :].astype(BF16)
    tail[...] = final[2:3, :].astype(BF16)


VM = pl.BlockSpec(memory_space=pltpu.VMEM)
SM = pl.BlockSpec(memory_space=pltpu.SMEM)
HB = pl.BlockSpec(memory_space=pl.ANY)
DMA = pltpu.SemaphoreType.DMA


def on_device(
    inputs, tail_inputs, states, tail_ids, routes, tail_routes, attention_gain,
    query_weight, key_weight, value_weight, decay_down, decay_up, decay_bias,
    decay_log, beta_weight, output_gain, head_out, expert_gain, router_weight,
    gate_weight, up_weight, down_weight,
):
    def vm(*dims, dtype=BF16):
        return pltpu.VMEM(dims, dtype)

    def both(lead, rest, sizes, dtype=BF16):
        return [vm(*lead, n, *rest, dtype=dtype) for n in sizes]

    heavy = (
        inputs, tail_inputs, states.reshape(R1, H, H), query_weight, key_weight,
        value_weight, decay_down, decay_up, head_out, router_weight, gate_weight,
        up_weight, down_weight,
    )
    scratch = [
        vm(R1, D), vm(R2, D), vm(R1, H, H), vm(D, 4 * H), vm(H, H), vm(H, D), vm(D, 128),
        vm(4, D, 2 * H), vm(4, H, D),
    ]
    scratch += [DMA((12,)), DMA((8,)), DMA((SEM_ROWS, 8))]
    scratch += [
        vm(RT, D), vm(R1, 8 * H, dtype=F32), vm(ND, R2, H), vm(R2, H, dtype=F32), vm(R1, 256, dtype=F32),
        vm(R1, H, dtype=F32), vm(R1, H, H), vm(R1, H, dtype=F32), vm(ND, R2, H), vm(ND, R2, H),
    ]
    t = (16, 128)
    scratch += both((NX,), t, TILES) + both((NX,), t, TILES)
    scratch += both((), t, TILES) + [vm(NZ, 3, *t), vm(NZ, 3, *t)]
    scratch += both((NX,), t, TILES) + both((NX,), t, TILES)
    scratch += both((), (D,), ROWS, F32)
    scratch += both((ND,), (D,), SLOTS) + both((ND,), (D,), SLOTS)
    scratch += both((4,), (D,), SLOTS) + both((4,), (D,), SLOTS) + both((4,), (D,), SLOTS)
    scratch += both((NX,), t, TILES) + both((NX,), t, TILES)
    scratch += both((), (D,), ROWS, F32)
    scratch += [vm(NZ * w, 128, dtype=F32) for w in OUTS]
    scratch += both((NZ,), (128,), OUTS) + both((NZ,), (128,), OUTS)
    scratch += [vm(8, D, dtype=F32)]
    final = pl.pallas_call(
        kernel,
        out_shape=jax.ShapeDtypeStruct((8, D), F32),
        in_specs=[HB] * 13 + [VM, VM, SM] + [VM] * 6,
        out_specs=VM,
        scratch_shapes=scratch,
        compiler_params=pltpu.CompilerParams(
            vmem_limit_bytes=VMEM_LIMIT, collective_id=0, has_side_effects=True
        ),
        name="two_steps",
    )(
        *heavy,
        attention_gain, decay_bias.reshape(1, H), decay_log,
        beta_weight.reshape(1, D), output_gain.reshape(1, H), expert_gain,
        tail_ids.reshape(1, 256), routes.T, tail_routes.T,
    )
    return pl.pallas_call(
        write_kernel,
        out_shape=(jax.ShapeDtypeStruct((2, D), BF16), jax.ShapeDtypeStruct((1, D), BF16)),
        in_specs=[VM],
        out_specs=(VM, VM),
        name="write",
    )(final)


def solution(mesh):
    placed = (
        P("dp", None),
        P("dp", None),
        P("dp", "expert", None, None),
        P(),
        P(),
        P(),
        P(),
        P(None, "expert"),
        P(None, "expert"),
        P(None, "expert"),
        P(),
        P(None, "expert"),
        P("expert"),
        P("expert"),
        P(None, "expert"),
        P(),
        P("expert", None),
        P(),
        P(),
        P("expert", None, "dp"),
        P("expert", None, "dp"),
        P("expert", "dp", None),
    )
    return jax.shard_map(
        on_device,
        mesh=mesh,
        in_specs=placed,
        out_specs=(P(("dp", "expert"), None), P(("dp", "expert"), None)),
        check_vma=False,
    )
```

```python
import functools

import jax
import jax.numpy as jnp
from jax import lax
from jax.experimental import pallas as pl
from jax.experimental.pallas import tpu as pltpu
from jax.sharding import PartitionSpec as P

F32 = jnp.float32
BF16 = jnp.bfloat16
EPS = 1e-06
ROUTE_SCALE = 2.446
MESH = pl.DeviceIdType.MESH
VMEM_LIMIT = 56 * 1024 * 1024
D = 2304
H = 128
NCT = D // 128
R1 = 64
R2 = 32
SECOND = 16
RT = R1 + R2
ND = 8
NX = 4
NZ = 8
ROWS = (64, 32)
SLOTS = (32, 16)
TILES = (18, 9)
OWNERS = (6, 3)
OUTS = (48, 32)
AX, AZ, BZ, BX, CC, DP, DY, EX, EZ = range(0, 18, 2)
KINDS = 18
PACK, HEAD = 2 * KINDS, 2 * KINDS + 2
SEM_ROWS = 2 * KINDS + 4


def iota(shape, dim):
    return lax.broadcasted_iota(jnp.int32, shape, dim)


def dot(a, b, contract=((1,), (0,)), precision=None):
    return lax.dot_general(
        a, b, (contract, ((), ())), precision=precision, preferred_element_type=F32
    )


def rms(wide, gain):
    factor = lax.rsqrt(jnp.mean(wide * wide, axis=-1, keepdims=True) + EPS)
    return wide * factor * gain


def cols(c):
    return slice(c * 128, c * 128 + 128)


def each(lo, hi, body):
    def step(k, carry):
        body(k)
        return carry

    lax.fori_loop(lo, hi, step, 0)


def kernel(
    x1h, x2h, sth, wqh, wkh, wvh, wddh, wduh, woh, roh, wgh, wuh, wdh,
    again, bias, dlog, wb, og, egain, ids, routes1, routes2,
    final,
    x1, x2, st, wall, wdu, wo, ro, wgu, wd,
    lsem, ssem, sem,
    normed, p1, p2all, w2, named, tp, fresh, h2s, h2c, h2r,
    ax_s1, ax_s2, ax_r1, ax_r2, az_s1, az_s2, az_r1, az_r2,
    rt1, rt2, hb1, hb2, hid1, hid2,
    slots1, slots2, out1, out2, pr1, pr2, zb1, zb2, zr1, zr2,
    ex_s1, ex_s2, ex_r1, ex_r2, res1, res2,
    scr1, scr2, ez_s1, ez_s2, ez_r1, ez_r2, rows,
):
    ax_s, ax_r, az_s, az_r = (ax_s1, ax_s2), (ax_r1, ax_r2), (az_s1, az_s2), (az_r1, az_r2)
    rt, hb, hid = (rt1, rt2), (hb1, hb2), (hid1, hid2)
    slots, out, pr, zb, zr = (slots1, slots2), (out1, out2), (pr1, pr2), (zb1, zb2), (zr1, zr2)
    ex_s, ex_r, res, scr = (ex_s1, ex_s2), (ex_r1, ex_r2), (res1, res2), (scr1, scr2)
    ez_s, ez_r = (ez_s1, ez_s2), (ez_r1, ez_r2)
    dp = lax.axis_index("dp")
    ex = lax.axis_index("expert")
    y = dp // 2
    core = lax.rem(dp, 2)
    xx = ex // NZ
    z = lax.rem(ex, NZ)

    def same(s):
        return 2 * lax.rem(y + s, 4) + core

    def other(s):
        return 2 * lax.rem(y + s, 4) + 1 - core

    def xat(s):
        return lax.rem(xx + s, NX)

    def zat(s):
        return lax.rem(z + s, NZ)

    def xdev(s):
        return {"expert": xat(s) * NZ + z}

    def zdev(s):
        return {"expert": xx * NZ + zat(s)}

    def rcopy(src, dst, row, snd, rcv, device):
        return pltpu.make_async_remote_copy(
            src_ref=src,
            dst_ref=dst,
            send_sem=sem.at[row, snd],
            recv_sem=sem.at[row + 1, rcv],
            device_id=device,
            device_id_type=MESH,
        )

    sent = []

    def send(make):
        make().start()
        sent.append(lambda: make().wait_send())

    def send_if(where, make):
        pl.when(where)(lambda: make().start())
        sent.append(lambda: pl.when(where)(lambda: make().wait_send()))

    loads = []
    for n, (src, dst) in enumerate(
        (
            (x2h, x2), (x1h, x1), (wqh, wall.at[:, pl.ds(0, H)]),
            (wkh, wall.at[:, pl.ds(H, H)]), (wvh, wall.at[:, pl.ds(2 * H, H)]),
            (wddh, wall.at[:, pl.ds(3 * H, H)]), (wduh, wdu),
        )
    ):
        loads.append(pltpu.make_async_copy(src, dst, lsem.at[n]))

    def load_state(i):
        part = pl.ds(i * 8, 8)
        return pltpu.make_async_copy(sth.at[part], st.at[part], ssem.at[i])

    later = []
    for n, (src, dst) in enumerate(((woh, wo), (roh, ro), (wgh, wgu.at[:, :, pl.ds(0, H)]), (wuh, wgu.at[:, :, pl.ds(H, H)]), (wdh, wd))):
        later.append(pltpu.make_async_copy(src, dst, lsem.at[7 + n]))
    for copy in loads:
        copy.start()
    barrier = pltpu.get_barrier_semaphore()
    for s in range(1, ND):
        pl.semaphore_signal(barrier, inc=1, device_id={"dp": lax.rem(dp + s, ND)}, device_id_type=MESH)
    for s in range(1, NX):
        pl.semaphore_signal(barrier, inc=1, device_id=xdev(s), device_id_type=MESH)
    for s in range(1, NZ):
        pl.semaphore_signal(barrier, inc=1, device_id=zdev(s), device_id_type=MESH)

    def load_block(k):
        block = xat(k + 1)
        load_state(2 * block).start()
        load_state(2 * block + 1).start()

    each(0, NX, load_block)
    later[0].start()
    load_wo, load_ro = later[0], later[1]

    again_row = again[...].reshape(1, D)
    egain_row = egain[...].reshape(1, D)
    for copy in loads[0:2]:
        copy.wait()
    normed[0:R1, :] = rms(x1[...].astype(F32), again_row).astype(BF16)
    normed[R1:RT, :] = rms(x2[...].astype(F32), again_row).astype(BF16)
    n = normed[...]
    beta = jax.nn.sigmoid(
        jnp.sum(n.astype(F32) * wb[...].astype(F32), axis=-1, keepdims=True)
    )
    for copy in loads[2:]:
        copy.wait()
    for copy in later[1:]:
        copy.start()
    every = dot(n, wall[...])

    def project(c):
        produced = every[:, cols(c)]
        return produced * jax.nn.sigmoid(produced)

    def unit(v):
        return v * lax.rsqrt(jnp.sum(v * v, axis=-1, keepdims=True) + EPS)

    q = unit(project(0))
    k = unit(project(1))
    v = project(2)
    low = every[:, cols(3)].astype(BF16)
    gate = dot(low, wdu[...]) + bias[...]
    soft = jnp.maximum(gate, 0.0) + jnp.log(1.0 + jnp.exp(-jnp.abs(gate)))
    strength = jnp.exp(jnp.full((RT, H), dlog[0], F32))
    decay = jnp.exp(-(strength * soft))
    dk = decay * k
    dq = decay * q
    sc = jnp.broadcast_to(beta * jnp.sum(k * q, axis=-1, keepdims=True), (RT, H))
    p2all[dp] = (dq - sc * dk)[R1:RT, :].astype(BF16)
    w2[...] = (sc * v)[R1:RT, :]
    pl.semaphore_wait(barrier, ND + NX + NZ - 3)

    def pack_copy(s, slot):
        return rcopy(
            p2all.at[dp], p2all.at[slot], PACK, s, slot, {"dp": lax.rem(dp + s, ND)}
        )

    each(1, ND, lambda s: pack_copy(s, dp).start())
    sent.append(lambda: each(1, ND, lambda s: pack_copy(s, dp).wait_send()))
    dk_hi = dk.astype(BF16).astype(F32)
    dq_hi = dq.astype(BF16).astype(F32)
    parts = (dk_hi, dk - dk_hi, dq_hi, dq - dq_hi, v, sc, decay, beta * k)
    for c, part in enumerate(parts):
        p1[:, cols(c)] = part[0:R1, :]

    m = iota((16, H), 0)

    def first_rows(start, count):
        t = p1[pl.ds(pl.multiple_of(start, count), count), :]
        dcol = jnp.transpose(t[:, cols(6)])
        bcol = jnp.transpose(t[:, cols(7)])
        reads = []
        for j in range(count):
            row = [t[j : j + 1, cols(c)] for c in range(6)]
            state = st[start + j]
            a = jnp.where(m == 0, row[0], jnp.where(m == 1, row[1], jnp.where(m == 2, row[2], row[3])))
            got = dot(a.astype(BF16), state)
            u = row[4] - (got[0:1] + got[1:2])
            reads.append(got[2:3] + got[3:4] + row[5] * u)
            fresh[start + j] = (
                state.astype(F32) * dcol[:, j : j + 1] + bcol[:, j : j + 1] * u
            ).astype(BF16)
        return rms(jnp.concatenate(reads, axis=0) * H**-0.5, og[...])

    order = iota((R1, R1), 0)
    within = order & 15
    source = order - within + jnp.where(within < 8, 2 * within, 2 * (within - 8) + 1)
    perm = (iota((R1, R1), 1) == source).astype(BF16)
    perm16 = perm[0:16, 0:16]

    def tile(p, val, xi, c):
        if p == 0:
            return val[xi * 16 : xi * 16 + 16, cols(c)]
        return jnp.concatenate(
            [val[xi * 8 : xi * 8 + 8, cols(2 * c)], val[xi * 8 : xi * 8 + 8, cols(2 * c + 1)]], axis=0
        )

    def a_send(p, val):
        for xi in range(NX):
            for c in range(TILES[p]):
                ax_s[p][xi, c] = tile(p, val, xi, c).astype(BF16)
        for s in (2, 1, 3):
            send(functools.partial(ax_copy, p, s, xx))

    def ax_copy(p, s, slot):
        return rcopy(ax_s[p].at[xat(s)], ax_r[p].at[slot], AX + KINDS * p, s, slot, xdev(s))

    def az_copy(p, s, slot):
        return rcopy(
            az_s[p].at[pl.ds(3 * zat(s), 3)], az_r[p].at[slot], AZ + KINDS * p, s, slot, zdev(s)
        )

    def az_own(p, slot):
        return rcopy(
            az_s[p].at[pl.ds(0, 3)], az_r[p].at[slot], AZ + KINDS * p, 0, slot, zdev(0)
        )

    def bz_copy(p, s, owner):
        part = hb[p].at[xx, pl.ds(3 * owner, 3)]
        return rcopy(part, part, BZ + KINDS * p, s, owner, zdev(s))

    def bx_copy(p, s, owner):
        part = hb[p].at[owner]
        return rcopy(part, part, BX + KINDS * p, s, owner, xdev(s))

    def a_turn(p):
        total = ax_s[p][xx].astype(F32)
        for s in (3, 2, 1):
            ax_copy(p, s, xat(s)).wait_recv()
            total = total + ax_r[p][xat(s)].astype(F32)
        az_s[p][...] = total.astype(BF16)
        for s in (4, 3, 5, 2, 6, 1, 7):
            send_if(zat(s) < OWNERS[p], functools.partial(az_copy, p, s, z))

    def b_start(p):
        @pl.when(z < OWNERS[p])
        def _():
            mine = pl.ds(3 * z, 3)
            total = az_s[p][mine].astype(F32) + rt[p][xx, mine].astype(F32)
            for s in (1, 7, 2, 6, 3, 5, 4):
                az_own(p, zat(s)).wait_recv()
                total = total + az_r[p][zat(s)].astype(F32)
            hb[p][xx, mine] = total.astype(BF16)
            for s in (4, 3, 5, 2, 6, 1, 7):
                bz_copy(p, s, z).start()

        def left():
            for s in range(1, NZ):
                bz_copy(p, s, z).wait_send()

        sent.append(lambda: pl.when(z < OWNERS[p])(left))

    def b_turn(p):
        for s in (1, 7, 2, 6, 3, 5, 4):

            @pl.when(zat(s) < OWNERS[p])
            def _():
                bz_copy(p, s, zat(s)).wait_recv()

        for s in (2, 1, 3):
            send(functools.partial(bx_copy, p, s, xx))

    def b_end(p):
        for s in (1, 3, 2):
            bx_copy(p, s, xat(s)).wait_recv()
        for xi in range(NX):
            for c in range(TILES[p]):
                got = hb[p][xi, c].astype(F32)
                if p == 0:
                    hid1[xi * 16 : xi * 16 + 16, cols(c)] = got
                else:
                    hid2[xi * 8 : xi * 8 + 8, cols(2 * c)] = got[0:8]
                    hid2[xi * 8 : xi * 8 + 8, cols(2 * c + 1)] = got[8:16]

    load_wo.wait()

    def first_x(k):
        s = lax.rem(k + 1, NX)
        xi = xat(s)
        load_state(2 * xi).wait()
        load_state(2 * xi + 1).wait()
        h16 = first_rows(xi * 16, 16).astype(BF16)
        val = dot(dot(perm16, h16).astype(BF16), wo[...])
        for c in range(NCT):
            ax_s1[xi, c] = val[:, cols(c)].astype(BF16)

        @pl.when(k < NX - 1)
        def _():
            ax_copy(0, s, xx).start()

    each(0, NX, first_x)
    sent.append(lambda: each(1, NX, lambda s: ax_copy(0, s, xx).wait_send()))

    xp = dot(perm, x1[...])
    x2v = x2[...].astype(F32)
    for xi in range(NX):
        for c in range(TILES[0]):
            rt1[xi, c] = tile(0, xp, xi, c).astype(BF16)
        for c in range(TILES[1]):
            rt2[xi, c] = tile(1, x2v, xi, c).astype(BF16)
    def multi_hot(tab, count):
        hot = jnp.zeros((count, 128), F32)
        for c in range(8):
            hot = hot + (tab[:, c : c + 1] == iota((count, 128), 1).astype(F32)).astype(F32)
        return hot

    def own_table(table, count):
        per = 128 // count
        lanes = pl.ds(pl.multiple_of(dp // per * 128, 128), 128)
        turned = jnp.transpose(table[:, lanes].astype(F32))
        got = turned[0:count]
        for g in range(1, per):
            got = jnp.where(lax.rem(dp, per) == g, turned[g * count : g * count + count], got)
        return got

    tab1, tab2 = own_table(routes1, R1), own_table(routes2, R2)
    mask = (dot(perm, multi_hot(tab1, R1).astype(BF16)), multi_hot(tab2, R2))
    expert_a, select, place = [], [], []
    for p in range(2):
        r, n_slots, cap = ROWS[p], SLOTS[p], (3, 2)[p]
        tri = (iota((r, r), 0) >= iota((r, r), 1)).astype(BF16)
        rank = (mask[p] * dot(tri, mask[p].astype(BF16))).astype(BF16)
        sa, sb = iota((128, n_slots), 1), iota((n_slots, 128), 0)
        hot_a = iota((128, n_slots), 0) == 4 * ex + (sa >> cap)
        hot_b = iota((n_slots, 128), 1) == 4 * ex + (sb >> cap)
        at_a = (iota((r, n_slots), 1) & ((1 << cap) - 1)) + 1
        at_b = (iota((n_slots, r), 0) & ((1 << cap) - 1)) + 1
        expert_a.append(hot_a.astype(F32))
        place.append((dot(rank, hot_a.astype(BF16)) == at_a.astype(F32)).astype(F32))
        select.append((dot(hot_b.astype(BF16), rank, ((1,), (1,))) == at_b.astype(F32)).astype(BF16))

    base = dp * R1
    named[...] = (ids[...] == base + iota((R1, 256), 0)).astype(F32)
    for s in range(1, ND):
        pack_copy(s, lax.rem(dp + s, ND)).wait_recv()
    tp[...] = dot(named[...].astype(BF16), p2all[...].reshape(ND * R2, H))

    def second_rows(k):
        count = SECOND
        at = pl.ds(pl.multiple_of(k * count, count), count)
        t = tp[at, :]
        reads = []
        for j in range(count):
            a = jnp.broadcast_to(t[j : j + 1], (16, H))
            reads.append(dot(a.astype(BF16), fresh[k * count + j])[0:1])
        h2s[at, :] = jnp.concatenate(reads, axis=0)

    each(0, R1 // SECOND, second_rows)
    h2c[...] = dot(named[...].astype(BF16), h2s[...].astype(BF16), ((0,), (0,))).astype(
        BF16
    ).reshape(ND, R2, H)

    def head_copy(s, slot):
        peer = lax.rem(dp + s, ND)
        return rcopy(h2c.at[peer], h2r.at[slot], HEAD, s, slot, {"dp": peer})

    each(1, ND, lambda s: head_copy(s, dp).start())
    sent.append(lambda: each(1, ND, lambda s: head_copy(s, dp).wait_send()))

    a_turn(0)
    for s in range(1, ND):
        head_copy(s, lax.rem(dp + s, ND)).wait_recv()
    h2r[dp] = h2c[dp]
    heads2 = h2r[0].astype(F32)
    for g in range(1, ND):
        heads2 = heads2 + h2r[g].astype(F32)
    heads2 = rms((heads2 + w2[...]) * H**-0.5, og[...])
    a_send(1, dot(heads2.astype(BF16), wo[...]))
    b_start(0)
    a_turn(1)
    b_turn(0)
    b_start(1)

    def c_copy(p, slot, row, device):
        part = slots[p].at[slot]
        return rcopy(part, part, CC + KINDS * p, row, slot, {"dp": device})

    def c_start(p):
        normed_p = rms(hid[p][...], egain_row).astype(BF16)
        slots[p][dp] = dot(select[p], normed_p).astype(BF16)
        for s in (2, 1, 3):
            send(functools.partial(c_copy, p, dp, s, same(s)))
        send(functools.partial(c_copy, p, dp, 0, other(0)))
        return normed_p

    def c_turn(p):
        for s in (1, 3, 2):
            c_copy(p, same(s), s, same(s)).wait_recv()
            send(functools.partial(c_copy, p, same(s), 3 + s, other(0)))

    def c_end(p):
        for s in (0, 1, 3, 2):
            c_copy(p, other(s), 0, other(0)).wait_recv()

    def weights(p, normed_p):
        scores = jax.nn.sigmoid(dot(normed_p, ro[...])) * mask[p]
        shares = ROUTE_SCALE * scores / jnp.sum(scores, axis=-1, keepdims=True)
        return dot(shares, expert_a[p], precision=lax.Precision.HIGHEST) * place[p]

    b_end(0)
    n0 = c_start(0)
    b_turn(1)
    load_ro.wait()
    w0 = weights(0, n0)
    b_end(1)
    n1 = c_start(1)
    w1 = weights(1, n1)
    share = (w0, w1)
    for copy in later[2:]:
        copy.wait()

    def hidden_units(x, e, mine):
        both = dot(x, wgu[e])
        g, u = both[:, 0:H], both[:, H : 2 * H]
        return jnp.where(mine, g * jax.nn.sigmoid(g) * u, 0.0).astype(BF16)

    spot = iota((ND * 16, H), 0) & 15

    def experts(p):
        if p == 0:
            for pair in range(2):
                x = slots1[:, 16 * pair : 16 * pair + 16, :].reshape(ND * 16, D)
                a0 = hidden_units(x, 2 * pair, (spot >> 3) == 0)
                a1 = hidden_units(x, 2 * pair + 1, (spot >> 3) == 1)
                for c in range(0, D, 768):
                    cc = slice(c, c + 768)
                    got = dot(a0, wd[2 * pair, :, cc]) + dot(a1, wd[2 * pair + 1, :, cc])
                    out1[:, 16 * pair : 16 * pair + 16, cc] = got.astype(BF16).reshape(ND, 16, 768)
        else:
            x = slots2[...].reshape(ND * 16, D)
            acts = [hidden_units(x, e, (spot >> 2) == e) for e in range(4)]
            for c in range(0, D, 768):
                cc = slice(c, c + 768)
                got = dot(acts[0], wd[0, :, cc])
                for e in range(1, 4):
                    got = got + dot(acts[e], wd[e, :, cc])
                out2[:, :, cc] = got.astype(BF16).reshape(ND, 16, 768)

    def pair_copy(p, s):
        yy = lax.rem(y + s, 4)
        return rcopy(out[p].at[other(s)], pr[p].at[yy], DP + KINDS * p, yy, yy, {"dp": other(0)})

    def chip_copy(p, s, slot):
        yy = lax.rem(y + s, 4)
        return rcopy(zb[p].at[yy], zr[p].at[slot], DY + KINDS * p, yy, slot, {"dp": same(s)})

    def d_start(p):
        for s in (2, 1, 3, 0):
            send(functools.partial(pair_copy, p, s))

    def d_turn(p):
        for s in (2, 1, 3):
            yy = lax.rem(y + s, 4)
            pair_copy(p, s).wait_recv()
            zb[p][yy] = (out[p][same(s)].astype(F32) + pr[p][yy].astype(F32)).astype(BF16)
            send(functools.partial(chip_copy, p, s, y))
        pair_copy(p, 0).wait_recv()

    def ex_copy(p, s, slot):
        return rcopy(ex_s[p].at[xat(s)], ex_r[p].at[slot], EX + KINDS * p, s, slot, xdev(s))

    def ez_copy(p, s, slot):
        return rcopy(ez_s[p].at[zat(s)], ez_r[p].at[slot], EZ + KINDS * p, s, slot, zdev(s))

    def e_start(p):
        total = out[p][dp].astype(F32) + pr[p][y].astype(F32)
        for s in (1, 3, 2):
            yy = lax.rem(y + s, 4)
            chip_copy(p, s, yy).wait_recv()
            total = total + zr[p][yy].astype(F32)
        summed = total.astype(BF16)
        w_hi = share[p].astype(BF16)
        w_lo = (share[p] - w_hi.astype(F32)).astype(BF16)
        got = dot(w_hi, summed) + dot(w_lo, summed)
        res[p][...] = got
        for xi in range(NX):
            for c in range(TILES[p]):
                ex_s[p][xi, c] = tile(p, got, xi, c).astype(BF16)
        for s in (2, 1, 3):
            send(functools.partial(ex_copy, p, s, xx))

    def e_turn(p):
        block = (16, 8)[p]
        at = pl.ds(pl.multiple_of(xx * block, block), block)
        own = (iota((block, 128), 0) & 7) == z
        for s in (1, 3, 2):
            ex_copy(p, s, xat(s)).wait_recv()
        scr[p][...] = jnp.zeros_like(scr[p])
        for c in range(TILES[p]):
            arrived = ex_r[p][xat(1), c].astype(F32)
            for s in (2, 3):
                arrived = arrived + ex_r[p][xat(s), c].astype(F32)
            for half in range(2):
                ct = c if p == 0 else 2 * c + half
                if p == 0 and half == 1:
                    continue
                mine = res[p][at, cols(ct)] + jnp.where(own, hid[p][at, cols(ct)], 0.0)
                if p == 0:
                    val = mine + arrived
                    scr1[pl.ds(ct, NZ, stride=48), :] = val[0:8]
                    scr1[pl.ds(NCT + ct, NZ, stride=48), :] = val[8:16]
                else:
                    scr2[pl.ds(ct, NZ, stride=32), :] = mine + arrived[8 * half : 8 * half + 8]
        w = OUTS[p]
        for zi in range(NZ):
            ez_s[p][zi] = scr[p][zi * w : zi * w + w, :].astype(BF16)
        for s in (4, 3, 5, 2, 6, 1, 7):
            send(functools.partial(ez_copy, p, s, z))

    def e_end(p):
        w = OUTS[p]
        total = scr[p][pl.ds(pl.multiple_of(z * w, w), w), :]
        for s in (1, 7, 2, 6, 3, 5, 4):
            ez_copy(p, s, zat(s)).wait_recv()
            total = total + ez_r[p][zat(s)].astype(F32)
        for j in range(2 - p):
            for ct in range(NCT):
                rows[2 * p + j : 2 * p + j + 1, cols(ct)] = total[j * NCT + ct : j * NCT + ct + 1, :]

    c_turn(0)
    c_end(0)
    experts(0)
    d_start(0)
    c_turn(1)
    d_turn(0)
    c_end(1)
    experts(1)
    d_start(1)
    d_turn(1)
    e_start(0)
    e_start(1)
    e_turn(0)
    e_turn(1)
    e_end(0)
    e_end(1)
    final[...] = rows[...]

    for left in sent:
        left()


def write_kernel(final, first, tail):
    first[...] = final[0:2, :].astype(BF16)
    tail[...] = final[2:3, :].astype(BF16)


VM = pl.BlockSpec(memory_space=pltpu.VMEM)
SM = pl.BlockSpec(memory_space=pltpu.SMEM)
HB = pl.BlockSpec(memory_space=pl.ANY)
DMA = pltpu.SemaphoreType.DMA


def on_device(
    inputs, tail_inputs, states, tail_ids, routes, tail_routes, attention_gain,
    query_weight, key_weight, value_weight, decay_down, decay_up, decay_bias,
    decay_log, beta_weight, output_gain, head_out, expert_gain, router_weight,
    gate_weight, up_weight, down_weight,
):
    def vm(*dims, dtype=BF16):
        return pltpu.VMEM(dims, dtype)

    def both(lead, rest, sizes, dtype=BF16):
        return [vm(*lead, n, *rest, dtype=dtype) for n in sizes]

    heavy = (
        inputs, tail_inputs, states.reshape(R1, H, H), query_weight, key_weight,
        value_weight, decay_down, decay_up, head_out, router_weight, gate_weight,
        up_weight, down_weight,
    )
    scratch = [
        vm(R1, D), vm(R2, D), vm(R1, H, H), vm(D, 4 * H), vm(H, H), vm(H, D), vm(D, 128),
        vm(4, D, 2 * H), vm(4, H, D),
    ]
    scratch += [DMA((12,)), DMA((8,)), DMA((SEM_ROWS, 8))]
    scratch += [
        vm(RT, D), vm(R1, 8 * H, dtype=F32), vm(ND, R2, H), vm(R2, H, dtype=F32), vm(R1, 256, dtype=F32),
        vm(R1, H, dtype=F32), vm(R1, H, H), vm(R1, H, dtype=F32), vm(ND, R2, H), vm(ND, R2, H),
    ]
    t = (16, 128)
    scratch += both((NX,), t, TILES) + both((NX,), t, TILES)
    scratch += both((), t, TILES) + [vm(NZ, 3, *t), vm(NZ, 3, *t)]
    scratch += both((NX,), t, TILES) + both((NX,), t, TILES)
    scratch += both((), (D,), ROWS, F32)
    scratch += both((ND,), (D,), SLOTS) + both((ND,), (D,), SLOTS)
    scratch += both((4,), (D,), SLOTS) + both((4,), (D,), SLOTS) + both((4,), (D,), SLOTS)
    scratch += both((NX,), t, TILES) + both((NX,), t, TILES)
    scratch += both((), (D,), ROWS, F32)
    scratch += [vm(NZ * w, 128, dtype=F32) for w in OUTS]
    scratch += both((NZ,), (128,), OUTS) + both((NZ,), (128,), OUTS)
    scratch += [vm(8, D, dtype=F32)]
    final = pl.pallas_call(
        kernel,
        out_shape=jax.ShapeDtypeStruct((8, D), F32),
        in_specs=[HB] * 13 + [VM, VM, SM] + [VM] * 6,
        out_specs=VM,
        scratch_shapes=scratch,
        compiler_params=pltpu.CompilerParams(
            vmem_limit_bytes=VMEM_LIMIT, collective_id=0, has_side_effects=True
        ),
        name="two_steps",
    )(
        *heavy,
        attention_gain, decay_bias.reshape(1, H), decay_log,
        beta_weight.reshape(1, D), output_gain.reshape(1, H), expert_gain,
        tail_ids.reshape(1, 256), routes.T, tail_routes.T,
    )
    return pl.pallas_call(
        write_kernel,
        out_shape=(jax.ShapeDtypeStruct((2, D), BF16), jax.ShapeDtypeStruct((1, D), BF16)),
        in_specs=[VM],
        out_specs=(VM, VM),
        name="write",
    )(final)


def solution(mesh):
    placed = (
        P("dp", None),
        P("dp", None),
        P("dp", "expert", None, None),
        P(),
        P(),
        P(),
        P(),
        P(None, "expert"),
        P(None, "expert"),
        P(None, "expert"),
        P(),
        P(None, "expert"),
        P("expert"),
        P("expert"),
        P(None, "expert"),
        P(),
        P("expert", None),
        P(),
        P(),
        P("expert", None, "dp"),
        P("expert", None, "dp"),
        P("expert", "dp", None),
    )
    return jax.shard_map(
        on_device,
        mesh=mesh,
        in_specs=placed,
        out_specs=(P(("dp", "expert"), None), P(("dp", "expert"), None)),
        check_vma=False,
    )
```
